512 devices in a mesh: dp: 512 (over y, x, z, core).
Axes of the slice: x: 4, y: 8, z: 8, core: 2. Of those that a mesh axis runs over, the one named last changes fastest.
Arguments:
- query_raw: bfloat16 [36864, 3584], P('dp'), may hold values from -1.25 to 1.25
- passage_raw: bfloat16 [36864, 3584], P('dp'), may hold values from -1.25 to 1.25
- pairing: int32 [512, 72], P('dp'), may hold values from 0 to 71, as said below
Outputs:
- losses: float32 [36864], P('dp')
- query_grad: float32 [36864, 3584], P('dp')
- passage_grad: float32 [36864, 3584], P('dp')
The draws below stay inside these ranges and needn't reach their ends.
Inputs may be any that keep to these rules, and one draw needn't show every extreme that they name: Row r of query block b is paired with row pairing[b, r] of passage block b; each row of pairing is a permutation of 0 to 71.
All inputs are finite; a program needn't handle non-finite values.
Results may differ from the reference program's by a relative error of at most 0.006.
Values may be sent and summed in bfloat16 or wider, within the bound.
No kernel may reach another device: no remote copies, remote signals or barrier semaphores. Data moves between devices by JAX's collectives and lax.ppermute only.
A program may use at most 64 MiB of HBM per device.

```python
import jax
import jax.numpy as jnp
from jax import lax

H = 3584
ROWS = 72
WINDOW = 3
NBLK = 512
TEXTS = 36864


def shared_parts(key):
    key_list = jax.random.split(key, 5)
    topics = jax.random.truncated_normal(key_list[0], -4.0, 4.0, (32, H), jnp.float32)
    topic_ids = jax.random.randint(key_list[1], (TEXTS,), 0, 32)
    pair_vectors = jax.random.truncated_normal(key_list[2], -4.0, 4.0, (TEXTS, H), jnp.float32)
    column_scale = jnp.exp(jax.random.uniform(key_list[3], (H,), jnp.float32, 0.0, jnp.log(10.0)))
    permuted = jax.vmap(lambda subkey: jax.random.permutation(subkey, ROWS))(jax.random.split(key_list[4], NBLK)).astype(jnp.int32)
    base_rows = 0.6 * jnp.take(topics, topic_ids, axis=0) + 0.8 * pair_vectors
    return (base_rows, column_scale, permuted)


def finish_rows(key, base_rows, column_scale):
    noise_key, row_key = jax.random.split(key)
    noise_rows = jax.random.truncated_normal(noise_key, -4.0, 4.0, (TEXTS, H), jnp.float32)
    vectors = base_rows + noise_rows
    row_scale = 0.5 * jnp.exp(jax.random.uniform(row_key, (TEXTS, 1), jnp.float32, 0.0, jnp.log(10.0)))
    return (0.002 * vectors * column_scale[None, :] * row_scale).astype(jnp.bfloat16)


def draw_pairing(key, part):
    base_rows, column_scale, permuted = shared_parts(key)
    return permuted


def draw_query_raw(key, part):
    base_rows, column_scale, permuted = shared_parts(key)
    key = jax.random.fold_in(key, 11)
    return finish_rows(key, base_rows, column_scale)


def draw_passage_raw(key, part):
    base_rows, column_scale, permuted = shared_parts(key)
    key = jax.random.fold_in(key, 13)
    inverse = jnp.argsort(permuted, axis=1).astype(jnp.int32)
    source_rows = (jnp.arange(NBLK, dtype=jnp.int32)[:, None] * ROWS + inverse).reshape(-1)
    return finish_rows(key, jnp.take(base_rows, source_rows, axis=0), column_scale)


def setup_inputs(seed: int = 0) -> dict:
    streams_of = jax.random.split(jax.random.key(seed), 4)
    query_raw = draw_query_raw(jax.random.fold_in(streams_of[3], 71), 0)
    passage_raw = draw_passage_raw(jax.random.fold_in(streams_of[3], 71), 0)
    pairing = draw_pairing(jax.random.fold_in(streams_of[3], 71), 0)
    return {"query_raw": query_raw, "passage_raw": passage_raw, "pairing": pairing}


INV_TEMP = 20.0
EPS = 1e-06

def unit_rows(raw_rows):
    widened = raw_rows.astype(jnp.float32)
    scale_rows = lax.rsqrt(lax.optimization_barrier(jnp.sum(widened * widened, axis=1, keepdims=True)) + EPS)
    return (widened * scale_rows, scale_rows)

def contract(left_rows, right_rows):
    return lax.dot_general(left_rows, right_rows, (((1,), (1,)), ((), ())), preferred_element_type=jnp.float32)

def expand(weight_rows, key_rows):
    return jnp.dot(weight_rows, key_rows, preferred_element_type=jnp.float32)

def similarity(left_rows, right_rows):
    return jnp.exp(INV_TEMP * contract(left_rows, right_rows) - INV_TEMP)

def centered(matrix):
    padding = jnp.zeros((matrix.shape[0], WINDOW * matrix.shape[1]), jnp.float32)
    return jnp.concatenate([padding, matrix, padding], axis=1)

def pairing_matrix(pair_row):
    return (pair_row[:, None] == jnp.arange(pair_row.shape[0], dtype=jnp.int32)[None, :]).astype(jnp.float32)

def normalize_loss(query_total, passage_total, paired, positive):
    normalizer = query_total + lax.optimization_barrier(jnp.sum(paired * passage_total[None, :], axis=1))
    reciprocal = 1.0 / normalizer
    passage_share = lax.optimization_barrier(jnp.sum(paired * reciprocal[:, None], axis=0))
    losses = jnp.log(normalizer) + INV_TEMP - positive
    return (reciprocal, passage_share, losses)

def raw_gradient(unit_data, scale_rows, gradient):
    return (gradient - unit_data * lax.optimization_barrier(jnp.sum(unit_data * gradient, axis=1, keepdims=True))) * scale_rows

def reference(query_raw, passage_raw, pairing):
    query_unit, query_scale = unit_rows(query_raw)
    passage_unit, passage_scale = unit_rows(passage_raw)
    query_low = query_unit.astype(jnp.bfloat16)
    passage_low = passage_unit.astype(jnp.bfloat16)
    feature_count = query_low.shape[1]
    query_blocks = query_low.reshape(NBLK, ROWS, feature_count)
    passage_blocks = passage_low.reshape(NBLK, ROWS, feature_count)
    window_span = 2 * WINDOW + 1
    offsets = jnp.arange(-WINDOW, WINDOW + 1, dtype=jnp.int32)
    eye_rows = jnp.eye(ROWS, dtype=jnp.float32)
    self_keep = 1.0 - centered(eye_rows)

    def gather_window(blocks, block_index):
        block_picks = ((block_index + offsets) % NBLK).astype(jnp.int32)
        return jnp.take(blocks, block_picks, axis=0).reshape((window_span * ROWS,) + blocks.shape[2:])

    def block_scores(block_index):
        query_own = query_blocks[block_index]
        passage_own = passage_blocks[block_index]
        query_keys = gather_window(query_blocks, block_index)
        passage_keys = gather_window(passage_blocks, block_index)
        paired = pairing_matrix(pairing[block_index])
        score_cross = INV_TEMP * contract(query_own, passage_keys)
        exp_cross = jnp.exp(score_cross - INV_TEMP)
        exp_queries = similarity(query_own, query_keys) * self_keep
        exp_passages = similarity(passage_own, passage_keys) * self_keep
        exp_reverse = similarity(passage_own, query_keys)
        return (query_keys, passage_keys, paired, score_cross, exp_cross, exp_queries, exp_passages, exp_reverse)

    def first_pass(block_index):
        query_keys, passage_keys, paired, score_cross, exp_cross, exp_queries, exp_passages, exp_reverse = block_scores(block_index)
        exp_kept = exp_reverse * (1.0 - centered(paired.T))
        query_total = lax.optimization_barrier(jnp.sum(exp_cross, axis=1)) + lax.optimization_barrier(jnp.sum(exp_queries, axis=1))
        passage_total = lax.optimization_barrier(jnp.sum(exp_passages, axis=1)) + lax.optimization_barrier(jnp.sum(exp_kept, axis=1))
        positive = lax.optimization_barrier(jnp.sum(centered(paired) * score_cross, axis=1))
        reciprocal, passage_share, losses = normalize_loss(query_total, passage_total, paired, positive)
        return jnp.stack([reciprocal, passage_share, losses])
    first_rows = lax.map(first_pass, jnp.arange(NBLK, dtype=jnp.int32))
    recip_blocks = first_rows[:, 0]
    share_blocks = first_rows[:, 1]
    losses = first_rows[:, 2].reshape(-1)

    def second_pass(block_index):
        query_keys, passage_keys, paired, score_cross, exp_cross, exp_queries, exp_passages, exp_reverse = block_scores(block_index)
        reciprocal = recip_blocks[block_index]
        passage_share = share_blocks[block_index]
        window_recip = gather_window(recip_blocks, block_index)
        window_share = gather_window(share_blocks, block_index)
        positive_center = centered(paired)
        pair_center = centered(paired.T)
        cross_rows = (exp_cross * reciprocal[:, None] - positive_center).astype(jnp.bfloat16)
        cross_cols = (exp_cross * (1.0 - positive_center) * window_share[None, :]).astype(jnp.bfloat16)
        query_rows = (exp_queries * reciprocal[:, None]).astype(jnp.bfloat16)
        query_cols = (exp_queries * window_recip[None, :]).astype(jnp.bfloat16)
        reverse_rows = (exp_reverse * (1.0 - pair_center) * passage_share[:, None]).astype(jnp.bfloat16)
        reverse_cols = (exp_reverse * window_recip[None, :] - pair_center).astype(jnp.bfloat16)
        passage_rows = (exp_passages * passage_share[:, None]).astype(jnp.bfloat16)
        passage_cols = (exp_passages * window_share[None, :]).astype(jnp.bfloat16)
        query_gradient = INV_TEMP * (expand(cross_rows, passage_keys) + expand(cross_cols, passage_keys) + expand(query_rows, query_keys) + expand(query_cols, query_keys))
        passage_gradient = INV_TEMP * (expand(reverse_cols, query_keys) + expand(reverse_rows, query_keys) + expand(passage_rows, passage_keys) + expand(passage_cols, passage_keys))
        return jnp.stack([query_gradient, passage_gradient])
    grad_blocks = lax.map(second_pass, jnp.arange(NBLK, dtype=jnp.int32))
    query_gradient = grad_blocks[:, 0].reshape(-1, feature_count)
    passage_gradient = grad_blocks[:, 1].reshape(-1, feature_count)
    query_grad = raw_gradient(query_unit, query_scale, query_gradient)
    passage_grad = raw_gradient(passage_unit, passage_scale, passage_gradient)
    return (losses, query_grad, passage_grad)
```

```python
import jax
import jax.numpy as jnp
from jax import lax
from jax.experimental import pallas as pl
from jax.experimental.pallas import tpu as pltpu
from jax.sharding import PartitionSpec as P

INV_TEMP = 20.0
EPS = 1e-06
TILE = 896
VMEM = pl.BlockSpec(memory_space=pltpu.VMEM)
HBM = pl.BlockSpec(memory_space=pl.ANY)


def contract(left_rows, right_rows):
    return lax.dot_general(
        left_rows, right_rows, (((1,), (1,)), ((), ())), preferred_element_type=jnp.float32
    )


def exp_score(score):
    return jnp.exp(INV_TEMP * score - INV_TEMP)


def eye_of(count):
    down = lax.broadcasted_iota(jnp.int32, (count, count), 0)
    across = lax.broadcasted_iota(jnp.int32, (count, count), 1)
    return (down == across).astype(jnp.float32)


def unit_kernel(query_any, passage_any, low_ref, scale_ref, query_ref, passage_ref, sems):
    copies = [
        pltpu.make_async_copy(query_any, query_ref, sems.at[0]),
        pltpu.make_async_copy(passage_any, passage_ref, sems.at[1]),
    ]
    for copy in copies:
        copy.start()
    for copy in copies:
        copy.wait()
    raw_rows = jnp.concatenate(
        [query_ref[...].astype(jnp.float32), passage_ref[...].astype(jnp.float32)], axis=0
    )
    scale_rows = lax.rsqrt(jnp.sum(raw_rows * raw_rows, axis=1, keepdims=True) + EPS)
    low_ref[...] = (raw_rows * scale_rows).astype(jnp.bfloat16)
    scale_ref[...] = scale_rows


def unit_rows(query_raw, passage_raw):
    rows, width = query_raw.shape
    return pl.pallas_call(
        unit_kernel,
        in_specs=[HBM, HBM],
        out_specs=(VMEM, VMEM),
        out_shape=(
            jax.ShapeDtypeStruct((2 * rows, width), jnp.bfloat16),
            jax.ShapeDtypeStruct((2 * rows, 1), jnp.float32),
        ),
        scratch_shapes=[
            pltpu.VMEM((rows, width), jnp.bfloat16),
            pltpu.VMEM((rows, width), jnp.bfloat16),
            pltpu.SemaphoreType.DMA((2,)),
        ],
        compiler_params=pltpu.CompilerParams(vmem_limit_bytes=121 * 2**19),
        cost_estimate=pl.CostEstimate(
            flops=6 * rows * width, bytes_accessed=8 * rows * width, transcendentals=0
        ),
        name="unit_rows",
    )(query_raw, passage_raw)


def first_far_kernel(own_ref, far_ref, mass_ref, score_ref, passed_ref):
    score_ref[...] = contract(own_ref[...], far_ref[...])
    passed_ref[...] = mass_ref[...]


def first_far(own, far, mass):
    count, width = own.shape
    square = jax.ShapeDtypeStruct((count, count), jnp.float32)
    return pl.pallas_call(
        first_far_kernel,
        in_specs=[VMEM] * 3,
        out_specs=(VMEM, VMEM),
        out_shape=(square, square),
        compiler_params=pltpu.CompilerParams(vmem_limit_bytes=16 * 2**20),
        cost_estimate=pl.CostEstimate(
            flops=2 * count * count * width, bytes_accessed=4 * count * width, transcendentals=0
        ),
        name="first_far",
    )(own, far, mass)


def total_kernel(
    partner_ref, own_ref, mate_ref, far_ref, far_score_ref, score_ref, mass_ref,
    mate_score_out, far_score_out, recip_ref, loss_ref,
):
    partner = partner_ref[...]
    eye = eye_of(partner.shape[0])
    own = own_ref[...]
    mate_score = contract(own, mate_ref[...])
    far_score = far_score_ref[...] + contract(own, far_ref[...])
    mate_score_out[...] = mate_score
    far_score_out[...] = far_score
    mass = mass_ref[...] + exp_score(mate_score) + exp_score(far_score)
    total_col = jnp.sum(mass, axis=1, keepdims=True)
    norm_row = jnp.sum((eye + partner) * total_col, axis=0, keepdims=True)
    recip_ref[...] = 1.0 / norm_row
    positive = jnp.sum(partner * score_ref[...], axis=0, keepdims=True)
    losses = jnp.log(norm_row) + INV_TEMP - INV_TEMP * positive
    loss_ref[...] = losses[:, : loss_ref.shape[1]]


def totals(partner, own, next_mate, far_second, far_score, own_score, mass):
    count, width = own.shape
    row = jax.ShapeDtypeStruct((1, count), jnp.float32)
    half_row = jax.ShapeDtypeStruct((1, count // 2), jnp.float32)
    square = jax.ShapeDtypeStruct((count, count), jnp.float32)
    return pl.pallas_call(
        total_kernel,
        in_specs=[VMEM] * 7,
        out_specs=(VMEM,) * 4,
        out_shape=(square, square, row, half_row),
        compiler_params=pltpu.CompilerParams(vmem_limit_bytes=16 * 2**20),
        cost_estimate=pl.CostEstimate(
            flops=4 * count * count * width,
            bytes_accessed=6 * count * width,
            transcendentals=2 * count * count,
        ),
        name="totals",
    )(partner, own, next_mate, far_second, far_score, own_score, mass)


def gradient_kernel(blocks, refs):
    partner_ref, scale_ref, own_row, mate_row, near_rows, next_rows, relay_rows = refs[:7]
    score_refs = refs[7 : 7 + blocks]
    key_refs = refs[7 + blocks : 8 + 2 * blocks]
    query_ref, passage_ref, query_out, passage_out, weight_ref, dot_ref = refs[8 + 2 * blocks :]
    count = partner_ref.shape[0]
    rows = count // 2
    step = pl.program_id(0)

    @pl.when(step == 0)
    def _():
        partner = partner_ref[...]
        eye = eye_of(count)
        recip_col = jnp.sum(eye * own_row[...], axis=1, keepdims=True)
        relayed = relay_rows[1:2, :]
        recip_rows = [
            own_row[...],
            mate_row[...],
            near_rows[0:1, :],
            near_rows[1:2, :],
            next_rows[0:1, :],
            next_rows[1:2, :],
            jnp.where(relayed > 0.0, relayed, next_rows[3:4, :]),
        ]
        along = jnp.zeros((count, count), jnp.float32)
        weights = []
        for index in range(blocks):
            score = score_refs[index][...]
            weight = exp_score(score) * (recip_col + recip_rows[index])
            if index == 0:
                weight = weight * (1.0 - eye) * (1.0 - 0.5 * partner) - partner
            low = weight.astype(jnp.bfloat16)
            along = along + low.astype(jnp.float32) * score
            weights.append(low)
        weight_ref[...] = jnp.concatenate(weights, axis=1)
        dot_ref[...] = INV_TEMP * jnp.sum(along, axis=1, keepdims=True)

    columns = pl.ds(pl.multiple_of(step * TILE, TILE), TILE)
    near_keys = [key_ref[:, columns] for key_ref in key_refs[: blocks - 1]]
    far_keys = key_refs[blocks - 1][:, columns] + key_refs[blocks][:, columns]
    keys = jnp.concatenate(near_keys + [far_keys], axis=0)
    gradient = jnp.dot(weight_ref[...], keys, preferred_element_type=jnp.float32)
    scale = scale_ref[...]
    along = dot_ref[...]
    for part, raw_ref, out_ref in ((0, query_ref, query_out), (1, passage_ref, passage_out)):
        span = slice(part * rows, (part + 1) * rows)
        unit = raw_ref[:, columns].astype(jnp.float32) * scale[span]
        out_ref[...] = (INV_TEMP * gradient[span] - unit * along[span]) * scale[span]


def gradients(partner, scale, recip_rows, scores, keys, query_raw, passage_raw):
    blocks = len(scores)
    rows, width = query_raw.shape
    count = 2 * rows
    out = jax.ShapeDtypeStruct((rows, width), jnp.float32)
    out_spec = pl.BlockSpec((rows, TILE), lambda step: (0, step))

    def body(*refs):
        gradient_kernel(blocks, refs)

    return pl.pallas_call(
        body,
        out_shape=(out, out),
        grid=(width // TILE,),
        in_specs=[VMEM] * (10 + 2 * blocks),
        out_specs=(out_spec, out_spec),
        scratch_shapes=[
            pltpu.VMEM((count, blocks * count), jnp.bfloat16),
            pltpu.VMEM((count, 1), jnp.float32),
        ],
        compiler_params=pltpu.CompilerParams(vmem_limit_bytes=32 * 2**20),
        cost_estimate=pl.CostEstimate(
            flops=2 * blocks * count * count * width,
            bytes_accessed=2 * blocks * count * width + 12 * rows * width,
            transcendentals=blocks * count * count,
        ),
        name="gradients",
    )(partner, scale, *recip_rows, *scores, *keys, query_raw, passage_raw)


def per_device(query_raw, passage_raw, pairing):
    size = lax.axis_size("dp")
    chips = size // 2
    rows = query_raw.shape[0]

    def swapped(value, partner_of):
        pairs = []
        for source in range(size):
            target = partner_of(source // 2, source % 2)
            if target is not None:
                pairs.append((source, (target[0] % chips) * 2 + target[1]))
        return lax.ppermute(value, "dp", pairs)

    def other_core(chip, core):
        return (chip, 1 - core)

    def near_chip(chip, core):
        return (chip ^ 1, core)

    def next_chip(chip, core):
        return (chip + 1 if chip % 2 else chip - 1, core)

    def far_over_next(chip, core):
        return (chip + 1 if core else chip - 1, 1 - core) if chip % 2 == core else None

    def far_over_near(chip, core):
        return (chip + 1 if core else chip - 1, 1 - core) if chip % 2 != core else None

    def near_from_direct(chip, core):
        return (chip ^ 1, core) if chip % 2 == core else None

    own, scale = unit_rows(query_raw, passage_raw)
    paired = (pairing[0][:, None] == jnp.arange(rows, dtype=jnp.int32)[None, :]).astype(jnp.float32)
    blank = jnp.zeros((rows, rows), jnp.float32)
    partner = jnp.block([[blank, paired], [paired.T, blank]])
    passage_row = jnp.arange(2 * rows)[:, None] >= rows
    keep = 1.0 - jnp.eye(2 * rows, dtype=jnp.float32) - jnp.where(passage_row, partner, 0.0)

    near = swapped(own, near_chip)
    next_block = swapped(own, next_chip)
    mate = swapped(own, other_core)
    far_first = swapped(near, far_over_next)
    near_mate = swapped(near, other_core)
    far_second = swapped(next_block, far_over_near)
    next_mate = swapped(next_block, other_core)

    keys = [own, mate, near, near_mate, next_block]
    scores = [contract(own, key) for key in keys]
    mass = exp_score(scores[0]) * keep
    for score in scores[1:]:
        mass = mass + exp_score(score)
    far_score, mass = first_far(own, far_first, mass)
    mate_score, far_score, recip, losses = totals(
        partner, own, next_mate, far_second, far_score, scores[0], mass
    )

    mate_row = swapped(recip, other_core)
    chip_rows = jnp.concatenate([recip, mate_row], axis=0)
    near_rows = swapped(chip_rows, near_chip)
    next_rows = swapped(jnp.concatenate([chip_rows, near_rows], axis=0), next_chip)
    relay_rows = swapped(next_rows, near_from_direct)

    query_grad, passage_grad = gradients(
        partner,
        scale,
        [recip, mate_row, near_rows, next_rows, relay_rows],
        scores + [mate_score, far_score],
        keys + [next_mate, far_first, far_second],
        query_raw,
        passage_raw,
    )
    return (losses.reshape(rows), query_grad, passage_grad)


def solution(mesh):
    in_specs = (P("dp", None), P("dp", None), P("dp", None))
    out_specs = (P("dp"), P("dp", None), P("dp", None))
    return jax.shard_map(
        per_device, mesh=mesh, in_specs=in_specs, out_specs=out_specs, check_vma=False
    )
```

```python
import jax
import jax.numpy as jnp
from jax import lax
from jax.experimental import pallas as pl
from jax.experimental.pallas import tpu as pltpu
from jax.sharding import PartitionSpec as P

INV_TEMP = 20.0
EPS = 1e-06
TILE = 896
RING = 16
VMEM = pl.BlockSpec(memory_space=pltpu.VMEM)
HBM = pl.BlockSpec(memory_space=pl.ANY)


def contract(left_rows, right_rows):
    return lax.dot_general(
        left_rows, right_rows, (((1,), (1,)), ((), ())), preferred_element_type=jnp.float32
    )


def exp_score(score):
    return jnp.exp(INV_TEMP * score - INV_TEMP)


def eye_of(count):
    down = lax.broadcasted_iota(jnp.int32, (count, count), 0)
    across = lax.broadcasted_iota(jnp.int32, (count, count), 1)
    return (down == across).astype(jnp.float32)


def unit_kernel(query_any, passage_any, low_ref, scale_ref, query_ref, passage_ref, sems):
    copies = [
        pltpu.make_async_copy(query_any, query_ref, sems.at[0]),
        pltpu.make_async_copy(passage_any, passage_ref, sems.at[1]),
    ]
    for copy in copies:
        copy.start()
    for copy in copies:
        copy.wait()
    raw_rows = jnp.concatenate(
        [query_ref[...].astype(jnp.float32), passage_ref[...].astype(jnp.float32)], axis=0
    )
    scale_rows = lax.rsqrt(jnp.sum(raw_rows * raw_rows, axis=1, keepdims=True) + EPS)
    low_ref[...] = (raw_rows * scale_rows).astype(jnp.bfloat16)
    scale_ref[...] = scale_rows


def unit_rows(query_raw, passage_raw):
    rows, width = query_raw.shape
    return pl.pallas_call(
        unit_kernel,
        in_specs=[HBM, HBM],
        out_specs=(VMEM, VMEM),
        out_shape=(
            jax.ShapeDtypeStruct((2 * rows, width), jnp.bfloat16),
            jax.ShapeDtypeStruct((2 * rows, 1), jnp.float32),
        ),
        scratch_shapes=[
            pltpu.VMEM((rows, width), jnp.bfloat16),
            pltpu.VMEM((rows, width), jnp.bfloat16),
            pltpu.SemaphoreType.DMA((2,)),
        ],
        compiler_params=pltpu.CompilerParams(vmem_limit_bytes=121 * 2**19),
        cost_estimate=pl.CostEstimate(
            flops=6 * rows * width, bytes_accessed=8 * rows * width, transcendentals=0
        ),
        name="unit_rows",
    )(query_raw, passage_raw)


def early_kernel(partner_ref, own_ref, mate_ref, near_ref, next_ref, *outs):
    *score_outs, mass_ref = outs
    partner = partner_ref[...]
    count = partner.shape[0]
    down = lax.broadcasted_iota(jnp.int32, (count, count), 0)
    keep = 1.0 - eye_of(count) - jnp.where(down >= count // 2, partner, 0.0)
    own = own_ref[...]
    mass = jnp.zeros((count, count), jnp.float32)
    for key_ref, score_out in zip((own_ref, mate_ref, near_ref, next_ref), score_outs):
        score = contract(own, key_ref[...])
        score_out[...] = score
        share = exp_score(score)
        mass = mass + (share * keep if key_ref is own_ref else share)
    mass_ref[...] = mass


def early_scores(partner, own, mate, near, next_block):
    count, width = own.shape
    square = jax.ShapeDtypeStruct((count, count), jnp.float32)
    return pl.pallas_call(
        early_kernel,
        in_specs=[VMEM] * 5,
        out_specs=(VMEM,) * 5,
        out_shape=(square,) * 5,
        compiler_params=pltpu.CompilerParams(vmem_limit_bytes=16 * 2**20),
        cost_estimate=pl.CostEstimate(
            flops=8 * count * count * width,
            bytes_accessed=8 * count * width,
            transcendentals=4 * count * count,
        ),
        name="early_scores",
    )(partner, own, mate, near, next_block)


def first_far_kernel(own_ref, far_ref, mass_ref, score_ref, passed_ref):
    score_ref[...] = contract(own_ref[...], far_ref[...])
    passed_ref[...] = mass_ref[...]


def first_far(own, far, mass):
    count, width = own.shape
    square = jax.ShapeDtypeStruct((count, count), jnp.float32)
    return pl.pallas_call(
        first_far_kernel,
        in_specs=[VMEM] * 3,
        out_specs=(VMEM, VMEM),
        out_shape=(square, square),
        compiler_params=pltpu.CompilerParams(vmem_limit_bytes=16 * 2**20),
        cost_estimate=pl.CostEstimate(
            flops=2 * count * count * width, bytes_accessed=4 * count * width, transcendentals=0
        ),
        name="first_far",
    )(own, far, mass)


def total_kernel(
    partner_ref, own_ref, near_mate_ref, next_mate_ref, far_ref, far_score_ref, score_ref, mass_ref,
    near_mate_out, next_mate_out, far_score_out, recip_ref, loss_ref,
):
    partner = partner_ref[...]
    eye = eye_of(partner.shape[0])
    own = own_ref[...]
    mass = mass_ref[...]
    for score, score_out in (
        (contract(own, near_mate_ref[...]), near_mate_out),
        (contract(own, next_mate_ref[...]), next_mate_out),
        (far_score_ref[...] + contract(own, far_ref[...]), far_score_out),
    ):
        score_out[...] = score
        mass = mass + exp_score(score)
    total_col = jnp.sum(mass, axis=1, keepdims=True)
    norm_row = jnp.sum((eye + partner) * total_col, axis=0, keepdims=True)
    recip_ref[...] = jnp.broadcast_to(1.0 / norm_row, recip_ref.shape)
    positive = jnp.sum(partner * score_ref[...], axis=0, keepdims=True)
    losses = jnp.log(norm_row) + INV_TEMP - INV_TEMP * positive
    loss_ref[...] = losses[:, : loss_ref.shape[1]]


def totals(partner, own, near_mate, next_mate, far_second, far_score, own_score, mass):
    count, width = own.shape
    spread = jax.ShapeDtypeStruct((RING, count), jnp.float32)
    half_row = jax.ShapeDtypeStruct((1, count // 2), jnp.float32)
    square = jax.ShapeDtypeStruct((count, count), jnp.float32)
    return pl.pallas_call(
        total_kernel,
        in_specs=[VMEM] * 8,
        out_specs=(VMEM,) * 5,
        out_shape=(square, square, square, spread, half_row),
        compiler_params=pltpu.CompilerParams(vmem_limit_bytes=16 * 2**20),
        cost_estimate=pl.CostEstimate(
            flops=6 * count * count * width,
            bytes_accessed=8 * count * width,
            transcendentals=3 * count * count,
        ),
        name="totals",
    )(partner, own, near_mate, next_mate, far_second, far_score, own_score, mass)


def gradient_kernel(blocks, refs):
    partner_ref, scale_ref, ring_rows, beyond_rows = refs[:4]
    score_refs = refs[4 : 4 + blocks]
    key_refs = refs[4 + blocks : 10 + blocks]
    first_ref, second_ref = refs[10 + blocks : 12 + blocks]
    query_ref, passage_ref, query_out, passage_out, weight_ref, dot_ref = refs[12 + blocks :]
    count = partner_ref.shape[0]
    rows = count // 2
    step = pl.program_id(0)

    @pl.when(step == 0)
    def _():
        partner = partner_ref[...]
        eye = eye_of(count)
        index = lax.axis_index("dp")
        place = lax.rem(index, RING)
        side = 1 - 2 * lax.rem(index, 2)
        turn = 2 - 4 * lax.rem(lax.div(index, 2), 2)

        def recip_row(offset):
            spot = place + offset
            wrapped = lax.rem(spot + RING, RING)
            inside = (spot >= 0) & (spot < RING)
            held = ring_rows[pl.ds(wrapped, 1), :]
            return jnp.where(inside, held, beyond_rows[pl.ds(wrapped, 1), :])

        recip_col = jnp.sum(eye * recip_row(0), axis=1, keepdims=True)
        offsets = [0, side, turn, -turn, turn + side, side - turn, -3 * side]
        along = jnp.zeros((count, count), jnp.float32)
        weights = []
        for index in range(blocks):
            score = score_refs[index][...]
            weight = exp_score(score) * (recip_col + recip_row(offsets[index]))
            if index == 0:
                weight = weight * (1.0 - eye) * (1.0 - 0.5 * partner) - partner
            low = weight.astype(jnp.bfloat16)
            along = along + low.astype(jnp.float32) * score
            weights.append(low)
        weight_ref[...] = jnp.concatenate(weights, axis=1)
        dot_ref[...] = INV_TEMP * jnp.sum(along, axis=1, keepdims=True)

    columns = pl.ds(pl.multiple_of(step * TILE, TILE), TILE)
    near_keys = [key_ref[:, columns] for key_ref in key_refs]
    far_keys = first_ref[:, columns] + second_ref[:, columns]
    keys = jnp.concatenate(near_keys + [far_keys], axis=0)
    gradient = jnp.dot(weight_ref[...], keys, preferred_element_type=jnp.float32)
    scale = scale_ref[...]
    along = dot_ref[...]
    for part, raw_ref, out_ref in ((0, query_ref, query_out), (1, passage_ref, passage_out)):
        span = slice(part * rows, (part + 1) * rows)
        unit = raw_ref[:, columns].astype(jnp.float32) * scale[span]
        out_ref[...] = (INV_TEMP * gradient[span] - unit * along[span]) * scale[span]


def gradients(partner, scale, ring_rows, beyond_rows, scores, keys, query_raw, passage_raw):
    blocks = len(scores)
    rows, width = query_raw.shape
    count = 2 * rows
    out = jax.ShapeDtypeStruct((rows, width), jnp.float32)
    out_spec = pl.BlockSpec((rows, TILE), lambda step: (0, step))

    def body(*refs):
        gradient_kernel(blocks, refs)

    return pl.pallas_call(
        body,
        out_shape=(out, out),
        grid=(width // TILE,),
        in_specs=[VMEM] * (14 + blocks),
        out_specs=(out_spec, out_spec),
        scratch_shapes=[
            pltpu.VMEM((count, blocks * count), jnp.bfloat16),
            pltpu.VMEM((count, 1), jnp.float32),
        ],
        compiler_params=pltpu.CompilerParams(vmem_limit_bytes=32 * 2**20),
        cost_estimate=pl.CostEstimate(
            flops=2 * blocks * count * count * width,
            bytes_accessed=2 * blocks * count * width + 12 * rows * width,
            transcendentals=blocks * count * count,
        ),
        name="gradients",
    )(partner, scale, ring_rows, beyond_rows, *scores, *keys, query_raw, passage_raw)


def per_device(query_raw, passage_raw, pairing):
    size = lax.axis_size("dp")
    chips = size // 2
    rows = query_raw.shape[0]

    def swapped(value, partner_of):
        pairs = []
        for source in range(size):
            target = partner_of(source // 2, source % 2)
            if target is not None:
                pairs.append((source, (target[0] % chips) * 2 + target[1]))
        return lax.ppermute(value, "dp", pairs)

    def other_core(chip, core):
        return (chip, 1 - core)

    def near_chip(chip, core):
        return (chip ^ 1, core)

    def next_chip(chip, core):
        return (chip + 1 if chip % 2 else chip - 1, core)

    def far_over_next(chip, core):
        return (chip + 1 if core else chip - 1, 1 - core) if chip % 2 == core else None

    def far_over_near(chip, core):
        return (chip + 1 if core else chip - 1, 1 - core) if chip % 2 != core else None

    def over_border(chip, core):
        place = 2 * chip % RING + core
        steps = {13: 5, 14: 2, 15: 2, 0: -2, 1: -2, 2: -5}
        if place not in steps:
            return None
        target = 2 * chip + core + steps[place]
        return (target // 2, target % 2)

    own, scale = unit_rows(query_raw, passage_raw)
    paired = (pairing[0][:, None] == jnp.arange(rows, dtype=jnp.int32)[None, :]).astype(jnp.float32)
    blank = jnp.zeros((rows, rows), jnp.float32)
    partner = jnp.block([[blank, paired], [paired.T, blank]])

    near = swapped(own, near_chip)
    next_block = swapped(own, next_chip)
    mate = swapped(own, other_core)
    far_first = swapped(near, far_over_next)
    far_second = swapped(next_block, far_over_near)
    near_mate = swapped(near, other_core)
    next_mate = swapped(next_block, other_core)

    *scores, mass = early_scores(partner, own, mate, near, next_block)
    far_score, mass = first_far(own, far_first, mass)
    *late_scores, spread, losses = totals(
        partner, own, near_mate, next_mate, far_second, far_score, scores[0], mass
    )

    groups = [list(range(start, start + RING)) for start in range(0, size, RING)]
    ring_rows = lax.all_to_all(
        spread, "dp", split_axis=0, concat_axis=0, axis_index_groups=groups, tiled=True
    )
    beyond_rows = swapped(ring_rows, over_border)

    query_grad, passage_grad = gradients(
        partner,
        scale,
        ring_rows,
        beyond_rows,
        scores + late_scores,
        [own, mate, near, next_block, near_mate, next_mate, far_first, far_second],
        query_raw,
        passage_raw,
    )
    return (losses.reshape(rows), query_grad, passage_grad)


def solution(mesh):
    in_specs = (P("dp", None), P("dp", None), P("dp", None))
    out_specs = (P("dp"), P("dp", None), P("dp", None))
    return jax.shard_map(
        per_device, mesh=mesh, in_specs=in_specs, out_specs=out_specs, check_vma=False
    )
```

```python
import functools

import jax
import jax.numpy as jnp
from jax import lax
from jax.experimental import pallas as pl
from jax.experimental.pallas import tpu as pltpu
from jax.sharding import PartitionSpec as P

INV_TEMP = 20.0
EPS = 1e-06
TILE = 896
SPREAD = 8
VMEM = pl.BlockSpec(memory_space=pltpu.VMEM)
HBM = pl.BlockSpec(memory_space=pl.ANY)


def contract(left_rows, right_rows):
    return lax.dot_general(
        left_rows, right_rows, (((1,), (1,)), ((), ())), preferred_element_type=jnp.float32
    )


def exp_score(score):
    return jnp.exp(INV_TEMP * score - INV_TEMP)


def eye_of(count):
    down = lax.broadcasted_iota(jnp.int32, (count, count), 0)
    across = lax.broadcasted_iota(jnp.int32, (count, count), 1)
    return (down == across).astype(jnp.float32)


def unit_kernel(
    query_any, passage_any, own_ref, first_ref, second_ref, scale_ref, query_ref, passage_ref, sems
):
    copies = [
        pltpu.make_async_copy(query_any, query_ref, sems.at[0]),
        pltpu.make_async_copy(passage_any, passage_ref, sems.at[1]),
    ]
    for copy in copies:
        copy.start()
    for copy in copies:
        copy.wait()
    raw_rows = jnp.concatenate(
        [query_ref[...].astype(jnp.float32), passage_ref[...].astype(jnp.float32)], axis=0
    )
    scale_rows = lax.rsqrt(jnp.sum(raw_rows * raw_rows, axis=1, keepdims=True) + EPS)
    low_rows = (raw_rows * scale_rows).astype(jnp.bfloat16)
    width = first_ref.shape[1]
    own_ref[...] = low_rows
    first_ref[...] = low_rows[:, :width]
    second_ref[...] = low_rows[:, width:]
    scale_ref[...] = scale_rows


def unit_rows(query_raw, passage_raw):
    rows, width = query_raw.shape
    whole = jax.ShapeDtypeStruct((2 * rows, width), jnp.bfloat16)
    half = jax.ShapeDtypeStruct((2 * rows, width // 2), jnp.bfloat16)
    return pl.pallas_call(
        unit_kernel,
        in_specs=[HBM, HBM],
        out_specs=(VMEM, VMEM, VMEM, VMEM),
        out_shape=(whole, half, half, jax.ShapeDtypeStruct((2 * rows, 1), jnp.float32)),
        scratch_shapes=[
            pltpu.VMEM((rows, width), jnp.bfloat16),
            pltpu.VMEM((rows, width), jnp.bfloat16),
            pltpu.SemaphoreType.DMA((2,)),
        ],
        compiler_params=pltpu.CompilerParams(vmem_limit_bytes=121 * 2**19),
        cost_estimate=pl.CostEstimate(
            flops=6 * rows * width, bytes_accessed=8 * rows * width, transcendentals=0
        ),
        name="unit_rows",
    )(query_raw, passage_raw)


def score_call(body, name, count, outs, operands, passed=()):
    size = sum(operand.size for operand in operands)
    return pl.pallas_call(
        body,
        in_specs=[VMEM] * len(operands),
        out_specs=[VMEM] * (len(outs) + len(passed)),
        out_shape=[jax.ShapeDtypeStruct(shape, jnp.float32) for shape in outs]
        + [jax.ShapeDtypeStruct(value.shape, value.dtype) for value in passed],
        compiler_params=pltpu.CompilerParams(vmem_limit_bytes=16 * 2**20),
        cost_estimate=pl.CostEstimate(
            flops=2 * count * size, bytes_accessed=2 * size, transcendentals=count * count
        ),
        name=name,
    )(*operands)


def halves_score(own, first, second):
    width = first.shape[1]
    return contract(own[:, :width], first) + contract(own[:, width:], second)


def early_kernel(
    partner_ref, own_ref, near_ref, next_first, next_second, *outs
):
    *score_outs, mass_ref, blank_ref, passed_ref = outs
    partner = partner_ref[...]
    count = partner.shape[0]
    down = lax.broadcasted_iota(jnp.int32, (count, count), 0)
    keep = 1.0 - eye_of(count) - jnp.where(down >= count // 2, partner, 0.0)
    own = own_ref[...]
    scores = [
        contract(own, own),
        contract(own, near_ref[...]),
        halves_score(own, next_first[...], next_second[...]),
    ]
    mass = exp_score(scores[0]) * keep
    for score in scores[1:]:
        mass = mass + exp_score(score)
    for score, score_out in zip(scores, score_outs):
        score_out[...] = score
    mass_ref[...] = mass
    blank_ref[...] = jnp.zeros((count, count), jnp.float32)
    passed_ref[...] = next_first[...]


def far_kernel(place, own_ref, far_ref, sum_ref, score_ref):
    width = far_ref.shape[1]
    own = own_ref[:, place * width : (place + 1) * width]
    score_ref[...] = sum_ref[...] + contract(own, far_ref[...])


def far_scores(own, far, score_sum, place):
    count = own.shape[0]
    body = functools.partial(far_kernel, place)
    return score_call(body, "far_scores", count, [(count, count)], [own, far, score_sum])[0]


def side_kernel(place, sum_ref, own_ref, key_ref, sum_out, score_out):
    width = key_ref.shape[1]
    sum_out[...] = sum_ref[...]
    score_out[...] = contract(own_ref[:, place * width : (place + 1) * width], key_ref[...])


def side_scores(own, key, score_sum, place):
    count = own.shape[0]
    body = functools.partial(side_kernel, place)
    return score_call(body, "side_scores", count, [(count, count)] * 2, [score_sum, own, key])


def total_kernel(
    far_score_ref, mass_ref, score_ref, partner_ref, own_ref, own_mate_score, near_mate_ref, mate_first, mate_second,
    near_mate_out, next_mate_out, recip_ref, spread_ref, loss_ref,
):
    partner = partner_ref[...]
    own = own_ref[...]
    mass = mass_ref[...] + exp_score(far_score_ref[...])
    mass = mass + exp_score(own_mate_score[...])
    near_score = contract(own, near_mate_ref[...])
    near_mate_out[...] = near_score
    mass = mass + exp_score(near_score)
    next_score = halves_score(own, mate_first[...], mate_second[...])
    next_mate_out[...] = next_score
    mass = mass + exp_score(next_score)
    total_col = jnp.sum(mass, axis=1, keepdims=True)
    eye = eye_of(partner.shape[0])
    norm_row = jnp.sum((eye + partner) * total_col, axis=0, keepdims=True)
    recip_ref[...] = 1.0 / norm_row
    spread_ref[...] = jnp.broadcast_to(1.0 / norm_row, spread_ref.shape)
    positive = jnp.sum(partner * score_ref[...], axis=0, keepdims=True)
    losses = jnp.log(norm_row) + INV_TEMP - INV_TEMP * positive
    loss_ref[...] = losses[:, : loss_ref.shape[1]]


def known_kernel(
    partner_ref, own_row, mate_row, far_row, own_score, mate_score, far_score, weight_ref, dot_ref
):
    partner = partner_ref[...]
    eye = eye_of(partner.shape[0])
    recip_col = jnp.sum(eye * own_row[...], axis=1, keepdims=True)
    along = jnp.zeros(partner.shape, jnp.float32)
    for index, (row_ref, score_ref) in enumerate(
        ((own_row, own_score), (mate_row, mate_score), (far_row, far_score))
    ):
        score = score_ref[...]
        weight = exp_score(score) * (recip_col + row_ref[0:1, :])
        if index == 0:
            weight = weight * (1.0 - eye) * (1.0 - 0.5 * partner) - partner
        low = weight.astype(jnp.bfloat16)
        along = along + low.astype(jnp.float32) * score
        weight_ref[index] = low
    dot_ref[...] = along


def known_weights(partner, rows, scores):
    count = partner.shape[0]
    return pl.pallas_call(
        known_kernel,
        in_specs=[VMEM] * 7,
        out_specs=(VMEM, VMEM),
        out_shape=(
            jax.ShapeDtypeStruct((3, count, count), jnp.bfloat16),
            jax.ShapeDtypeStruct((count, count), jnp.float32),
        ),
        compiler_params=pltpu.CompilerParams(vmem_limit_bytes=16 * 2**20),
        cost_estimate=pl.CostEstimate(
            flops=40 * count * count,
            bytes_accessed=32 * count * count,
            transcendentals=3 * count * count,
        ),
        name="known_weights",
    )(partner, *rows, *scores)


def gradient_kernel(
    known_ref, along_ref, scale_ref, own_row, next_rows, near_rows, *refs
):
    score_refs = refs[:4]
    own_ref, mate_ref, near_ref, near_mate, far_first = refs[4:9]
    half_refs = refs[9:12], refs[12:15]
    query_ref, passage_ref, query_out, passage_out, weight_ref, dot_ref = refs[15:]
    count = along_ref.shape[0]
    rows = count // 2
    step = pl.program_id(0)

    @pl.when(step == 0)
    def _():
        recip_col = jnp.sum(eye_of(count) * own_row[...], axis=1, keepdims=True)
        along = along_ref[...]
        recip_rows = [near_rows[0:1, :], next_rows[0:1, :], near_rows[1:2, :], next_rows[1:2, :]]
        weights = [known_ref[0], known_ref[1]]
        for score_ref, recip_row in zip(score_refs, recip_rows):
            score = score_ref[...]
            low = (exp_score(score) * (recip_col + recip_row)).astype(jnp.bfloat16)
            along = along + low.astype(jnp.float32) * score
            weights.append(low)
        weights.append(known_ref[2])
        weight_ref[...] = jnp.concatenate(weights, axis=1)
        dot_ref[...] = INV_TEMP * jnp.sum(along, axis=1, keepdims=True)

    half_steps = pl.num_programs(0) // 2
    whole = pl.ds(pl.multiple_of(step * TILE, TILE), TILE)

    def emit(half):
        next_ref, next_mate, far_second = half_refs[half]
        columns = pl.ds(pl.multiple_of((step - half * half_steps) * TILE, TILE), TILE)
        keys = [
            own_ref[:, whole],
            mate_ref[:, whole],
            near_ref[:, whole],
            next_ref[:, columns],
            near_mate[:, whole],
            next_mate[:, columns],
            far_first[:, whole] + far_second[:, columns],
        ]
        keys = jnp.concatenate(keys, axis=0)
        gradient = jnp.dot(weight_ref[...], keys, preferred_element_type=jnp.float32)
        scale = scale_ref[...]
        along = dot_ref[...]
        for part, raw_ref, out_ref in ((0, query_ref, query_out), (1, passage_ref, passage_out)):
            span = slice(part * rows, (part + 1) * rows)
            unit = raw_ref[:, whole].astype(jnp.float32) * scale[span]
            out_ref[...] = (INV_TEMP * gradient[span] - unit * along[span]) * scale[span]

    @pl.when(step < half_steps)
    def _():
        emit(0)

    @pl.when(step >= half_steps)
    def _():
        emit(1)


def gradients(known, scale, recip_rows, scores, keys, query_raw, passage_raw):
    blocks = 7
    rows, width = query_raw.shape
    count = 2 * rows
    out = jax.ShapeDtypeStruct((rows, width), jnp.float32)
    out_spec = pl.BlockSpec((rows, TILE), lambda step: (0, step))

    return pl.pallas_call(
        gradient_kernel,
        out_shape=(out, out),
        grid=(width // TILE,),
        in_specs=[VMEM] * (12 + len(scores) + len(keys) - 4),
        out_specs=(out_spec, out_spec),
        scratch_shapes=[
            pltpu.VMEM((count, blocks * count), jnp.bfloat16),
            pltpu.VMEM((count, 1), jnp.float32),
        ],
        compiler_params=pltpu.CompilerParams(vmem_limit_bytes=32 * 2**20),
        cost_estimate=pl.CostEstimate(
            flops=2 * blocks * count * count * width,
            bytes_accessed=2 * blocks * count * width + 12 * rows * width,
            transcendentals=blocks * count * count,
        ),
        name="gradients",
    )(*known, scale, *recip_rows, *scores, *keys, query_raw, passage_raw)


def per_device(query_raw, passage_raw, pairing):
    size = lax.axis_size("dp")
    chips = size // 2
    rows = query_raw.shape[0]

    def swapped(value, partner_of):
        pairs = []
        for source in range(size):
            target = partner_of(source // 2, source % 2)
            if target is not None:
                pairs.append((source, (target[0] % chips) * 2 + target[1]))
        return lax.ppermute(value, "dp", pairs)

    def other_core(chip, core):
        return (chip, 1 - core)

    def near_chip(chip, core):
        return (chip ^ 1, core)

    def next_chip(chip, core):
        return (chip + 1 if chip % 2 else chip - 1, core)

    def far_over_next(chip, core):
        return (chip + 1 if core else chip - 1, 1 - core) if chip % 2 == core else None

    def far_over_near(chip, core):
        return (chip + 1 if core else chip - 1, 1 - core) if chip % 2 != core else None

    def chip_beyond(chip, core):
        return (chip + 2 if core else chip - 2, 1 - core)

    own, first, second, scale = unit_rows(query_raw, passage_raw)
    paired = (pairing[0][:, None] == jnp.arange(rows, dtype=jnp.int32)[None, :]).astype(jnp.float32)
    blank = jnp.zeros((rows, rows), jnp.float32)
    partner = jnp.block([[blank, paired], [paired.T, blank]])

    near = swapped(own, near_chip)
    next_halves = [swapped(half, next_chip) for half in (first, second)]
    mate = swapped(own, other_core)
    far_first = swapped(near, far_over_next)
    far_second = [swapped(half, far_over_near) for half in next_halves]
    near_mate = swapped(near, other_core)

    count = 2 * rows
    square = (count, count)
    *scores, mass, far_score, passed = score_call(
        early_kernel,
        "early_scores",
        count,
        [square] * 5,
        [partner, own, near, *next_halves],
        [next_halves[0]],
    )
    next_mate = [swapped(half, other_core) for half in (passed, next_halves[1])]
    far_score, mate_score = side_scores(own, mate, far_score, 0)
    far_score = far_scores(own, far_second[0], far_score, 0)
    far_score = far_scores(own, far_second[1], far_score, 1)
    far_score = far_scores(own, far_first, far_score, 0)
    near_mate_score, next_mate_score, recip, spread, losses = score_call(
        total_kernel,
        "totals",
        count,
        [square, square, (1, count), (SPREAD, count), (1, rows)],
        [far_score, mass, scores[0], partner, own, mate_score, near_mate, *next_mate],
    )

    mate_row = swapped(recip, other_core)
    chip_rows = jnp.concatenate([recip, mate_row], axis=0)
    next_rows = swapped(chip_rows, next_chip)
    near_rows = swapped(chip_rows, near_chip)
    far_row = swapped(spread, chip_beyond)

    known = known_weights(partner, [recip, mate_row, far_row], [scores[0], mate_score, far_score])
    query_grad, passage_grad = gradients(
        known,
        scale,
        [recip, next_rows, near_rows],
        scores[1:] + [near_mate_score, next_mate_score],
        [own, mate, near, near_mate, far_first]
        + [next_halves[0], next_mate[0], far_second[0]]
        + [next_halves[1], next_mate[1], far_second[1]],
        query_raw,
        passage_raw,
    )
    return (losses.reshape(rows), query_grad, passage_grad)


def solution(mesh):
    in_specs = (P("dp", None), P("dp", None), P("dp", None))
    out_specs = (P("dp"), P("dp", None), P("dp", None))
    return jax.shard_map(
        per_device, mesh=mesh, in_specs=in_specs, out_specs=out_specs, check_vma=False
    )
```

```python
import functools

import jax
import jax.numpy as jnp
from jax import lax
from jax.experimental import pallas as pl
from jax.experimental.pallas import tpu as pltpu
from jax.sharding import PartitionSpec as P

INV_TEMP = 20.0
EPS = 1e-06
TILE = 896
SPREAD = 8
VMEM = pl.BlockSpec(memory_space=pltpu.VMEM)
HBM = pl.BlockSpec(memory_space=pl.ANY)


def contract(left_rows, right_rows):
    return lax.dot_general(
        left_rows, right_rows, (((1,), (1,)), ((), ())), preferred_element_type=jnp.float32
    )


def exp_score(score):
    return jnp.exp(INV_TEMP * score - INV_TEMP)


def eye_of(count):
    down = lax.broadcasted_iota(jnp.int32, (count, count), 0)
    across = lax.broadcasted_iota(jnp.int32, (count, count), 1)
    return (down == across).astype(jnp.float32)


def unit_kernel(
    query_any, passage_any, own_ref, first_ref, second_ref, scale_ref, query_ref, passage_ref, sems
):
    copies = [
        pltpu.make_async_copy(query_any, query_ref, sems.at[0]),
        pltpu.make_async_copy(passage_any, passage_ref, sems.at[1]),
    ]
    for copy in copies:
        copy.start()
    for copy in copies:
        copy.wait()
    raw_rows = jnp.concatenate(
        [query_ref[...].astype(jnp.float32), passage_ref[...].astype(jnp.float32)], axis=0
    )
    scale_rows = lax.rsqrt(jnp.sum(raw_rows * raw_rows, axis=1, keepdims=True) + EPS)
    low_rows = (raw_rows * scale_rows).astype(jnp.bfloat16)
    width = first_ref.shape[1]
    own_ref[...] = low_rows
    first_ref[...] = low_rows[:, :width]
    second_ref[...] = low_rows[:, width:]
    scale_ref[...] = scale_rows


def unit_rows(query_raw, passage_raw):
    rows, width = query_raw.shape
    whole = jax.ShapeDtypeStruct((2 * rows, width), jnp.bfloat16)
    half = jax.ShapeDtypeStruct((2 * rows, width // 2), jnp.bfloat16)
    return pl.pallas_call(
        unit_kernel,
        in_specs=[HBM, HBM],
        out_specs=(VMEM, VMEM, VMEM, VMEM),
        out_shape=(whole, half, half, jax.ShapeDtypeStruct((2 * rows, 1), jnp.float32)),
        scratch_shapes=[
            pltpu.VMEM((rows, width), jnp.bfloat16),
            pltpu.VMEM((rows, width), jnp.bfloat16),
            pltpu.SemaphoreType.DMA((2,)),
        ],
        compiler_params=pltpu.CompilerParams(vmem_limit_bytes=121 * 2**19),
        cost_estimate=pl.CostEstimate(
            flops=6 * rows * width, bytes_accessed=8 * rows * width, transcendentals=0
        ),
        name="unit_rows",
    )(query_raw, passage_raw)


def score_call(body, name, count, outs, operands, passed=()):
    size = sum(operand.size for operand in operands)
    return pl.pallas_call(
        body,
        in_specs=[VMEM] * len(operands),
        out_specs=[VMEM] * (len(outs) + len(passed)),
        out_shape=[jax.ShapeDtypeStruct(shape, jnp.float32) for shape in outs]
        + [jax.ShapeDtypeStruct(value.shape, value.dtype) for value in passed],
        compiler_params=pltpu.CompilerParams(vmem_limit_bytes=16 * 2**20),
        cost_estimate=pl.CostEstimate(
            flops=2 * count * size, bytes_accessed=2 * size, transcendentals=count * count
        ),
        name=name,
    )(*operands)


def halves_score(own, first, second):
    width = first.shape[1]
    return contract(own[:, :width], first) + contract(own[:, width:], second)


def early_kernel(
    partner_ref, own_ref, near_ref, next_first, next_second, *outs
):
    *score_outs, mass_ref, blank_ref, passed_ref = outs
    partner = partner_ref[...]
    count = partner.shape[0]
    down = lax.broadcasted_iota(jnp.int32, (count, count), 0)
    keep = 1.0 - eye_of(count) - jnp.where(down >= count // 2, partner, 0.0)
    own = own_ref[...]
    scores = [
        contract(own, own),
        contract(own, near_ref[...]),
        halves_score(own, next_first[...], next_second[...]),
    ]
    mass = exp_score(scores[0]) * keep
    for score in scores[1:]:
        mass = mass + exp_score(score)
    for score, score_out in zip(scores, score_outs):
        score_out[...] = score
    mass_ref[...] = mass
    blank_ref[...] = jnp.zeros((count, count), jnp.float32)
    passed_ref[...] = next_first[...]


def far_kernel(place, own_ref, far_ref, sum_ref, score_ref):
    width = far_ref.shape[1]
    own = own_ref[:, place * width : (place + 1) * width]
    score_ref[...] = sum_ref[...] + contract(own, far_ref[...])


def far_scores(own, far, score_sum, place):
    count = own.shape[0]
    body = functools.partial(far_kernel, place)
    return score_call(body, "far_scores", count, [(count, count)], [own, far, score_sum])[0]


def side_kernel(place, sum_ref, own_ref, key_ref, sum_out, score_out):
    width = key_ref.shape[1]
    sum_out[...] = sum_ref[...]
    score_out[...] = contract(own_ref[:, place * width : (place + 1) * width], key_ref[...])


def side_scores(own, key, score_sum, place):
    count = own.shape[0]
    body = functools.partial(side_kernel, place)
    return score_call(body, "side_scores", count, [(count, count)] * 2, [score_sum, own, key])


def total_kernel(
    far_score_ref, mass_ref, score_ref, partner_ref, own_ref, own_mate_score, near_mate_ref, mate_first, mate_second,
    near_mate_out, next_mate_out, recip_ref, spread_ref, loss_ref,
):
    partner = partner_ref[...]
    own = own_ref[...]
    mass = mass_ref[...] + exp_score(far_score_ref[...])
    mass = mass + exp_score(own_mate_score[...])
    near_score = contract(own, near_mate_ref[...])
    near_mate_out[...] = near_score
    mass = mass + exp_score(near_score)
    next_score = halves_score(own, mate_first[...], mate_second[...])
    next_mate_out[...] = next_score
    mass = mass + exp_score(next_score)
    total_col = jnp.sum(mass, axis=1, keepdims=True)
    eye = eye_of(partner.shape[0])
    norm_row = jnp.sum((eye + partner) * total_col, axis=0, keepdims=True)
    recip_ref[...] = 1.0 / norm_row
    spread_ref[...] = jnp.broadcast_to(1.0 / norm_row, spread_ref.shape)
    positive = jnp.sum(partner * score_ref[...], axis=0, keepdims=True)
    losses = jnp.log(norm_row) + INV_TEMP - INV_TEMP * positive
    loss_ref[...] = losses[:, : loss_ref.shape[1]]


def weigh(score, recip_col, recip_row):
    weight = exp_score(score) * (recip_col + recip_row)
    low = weight.astype(jnp.bfloat16)
    return low, low.astype(jnp.float32) * score


def column_of(row):
    return jnp.sum(eye_of(row.shape[1]) * row, axis=1, keepdims=True)


def part_kernel(
    partner_ref, own_row, mate_row, far_row, next_rows, own_score, mate_score, far_score, next_score,
    next_mate_score, own_ref, mate_ref, far_first, far_0, far_1, next_0, next_1, pair_0, pair_1,
    sum_ref, along_ref,
):
    partner = partner_ref[...]
    count = partner.shape[0]
    recip_row = own_row[...]
    recip_col = column_of(recip_row)
    score = own_score[...]
    weight = exp_score(score) * (recip_col + recip_row)
    weight = weight * (1.0 - eye_of(count)) * (1.0 - 0.5 * partner) - partner
    low = weight.astype(jnp.bfloat16)
    weights = [low]
    along = low.astype(jnp.float32) * score
    for score_ref, row in (
        (mate_score, mate_row[...]),
        (far_score, far_row[0:1, :]),
        (next_score, next_rows[0:1, :]),
        (next_mate_score, next_rows[1:2, :]),
    ):
        low, share = weigh(score_ref[...], recip_col, row)
        weights.append(low)
        along = along + share
    along_ref[...] = along
    weights = jnp.concatenate(weights, axis=1)
    half = next_0.shape[1]
    for start in range(0, own_ref.shape[1], TILE):
        whole = slice(start, start + TILE)
        columns = slice(start % half, start % half + TILE)
        far_ref, next_ref, pair_ref = ((far_0, next_0, pair_0), (far_1, next_1, pair_1))[start // half]
        keys = [
            own_ref[:, whole],
            mate_ref[:, whole],
            far_first[:, whole] + far_ref[:, columns],
            next_ref[:, columns],
            pair_ref[:, columns],
        ]
        keys = jnp.concatenate(keys, axis=0)
        sum_ref[:, whole] = jnp.dot(weights, keys, preferred_element_type=jnp.float32)


def part_gradients(partner, rows, scores, keys):
    count = partner.shape[0]
    width = keys[0].shape[1]
    operands = [partner, *rows, *scores, *keys]
    return pl.pallas_call(
        part_kernel,
        in_specs=[VMEM] * len(operands),
        out_specs=(VMEM, VMEM),
        out_shape=(
            jax.ShapeDtypeStruct((count, width), jnp.float32),
            jax.ShapeDtypeStruct((count, count), jnp.float32),
        ),
        compiler_params=pltpu.CompilerParams(vmem_limit_bytes=24 * 2**20),
        cost_estimate=pl.CostEstimate(
            flops=10 * count * count * width,
            bytes_accessed=16 * count * width,
            transcendentals=5 * count * count,
        ),
        name="part_gradients",
    )(*operands)


def gradient_kernel(
    sum_ref, along_ref, scale_ref, own_row, near_rows, near_score, pair_score, near_ref, pair_ref,
    query_ref, passage_ref, query_out, passage_out, query_hold, passage_hold, sems,
):
    count = along_ref.shape[0]
    rows = count // 2
    recip_col = column_of(own_row[...])
    near_low, near_share = weigh(near_score[...], recip_col, near_rows[0:1, :])
    pair_low, pair_share = weigh(pair_score[...], recip_col, near_rows[1:2, :])
    along = along_ref[...] + near_share + pair_share
    along = INV_TEMP * jnp.sum(along, axis=1, keepdims=True)
    weights = jnp.concatenate([near_low, pair_low], axis=1)
    scale = scale_ref[...]
    copies = []
    for start in range(0, near_ref.shape[1], TILE):
        whole = slice(start, start + TILE)
        keys = jnp.concatenate([near_ref[:, whole], pair_ref[:, whole]], axis=0)
        gradient = jnp.dot(weights, keys, preferred_element_type=jnp.float32) + sum_ref[:, whole]
        for part, raw_ref, hold, out in (
            (0, query_ref, query_hold, query_out),
            (1, passage_ref, passage_hold, passage_out),
        ):
            span = slice(part * rows, (part + 1) * rows)
            unit = raw_ref[:, whole].astype(jnp.float32) * scale[span]
            hold[:, whole] = (INV_TEMP * gradient[span] - unit * along[span]) * scale[span]
            copy = pltpu.make_async_copy(
                hold.at[:, whole], out.at[:, whole], sems.at[len(copies)]
            )
            copy.start()
            copies.append(copy)
    for copy in copies:
        copy.wait()


def gradients(part_sum, along, scale, rows, scores, keys, query_raw, passage_raw):
    count, width = part_sum.shape
    out = jax.ShapeDtypeStruct((count // 2, width), jnp.float32)
    operands = [part_sum, along, scale, *rows, *scores, *keys, query_raw, passage_raw]
    return pl.pallas_call(
        gradient_kernel,
        in_specs=[VMEM] * len(operands),
        out_specs=(HBM, HBM),
        out_shape=(out, out),
        scratch_shapes=[
            pltpu.VMEM((count // 2, width), jnp.float32),
            pltpu.VMEM((count // 2, width), jnp.float32),
            pltpu.SemaphoreType.DMA((2 * width // TILE,)),
        ],
        compiler_params=pltpu.CompilerParams(vmem_limit_bytes=24 * 2**20),
        cost_estimate=pl.CostEstimate(
            flops=4 * count * count * width,
            bytes_accessed=12 * count * width,
            transcendentals=2 * count * count,
        ),
        name="gradients",
    )(*operands)


def per_device(query_raw, passage_raw, pairing):
    size = lax.axis_size("dp")
    chips = size // 2
    rows = query_raw.shape[0]

    def swapped(value, partner_of):
        pairs = []
        for source in range(size):
            target = partner_of(source // 2, source % 2)
            if target is not None:
                pairs.append((source, (target[0] % chips) * 2 + target[1]))
        return lax.ppermute(value, "dp", pairs)

    def other_core(chip, core):
        return (chip, 1 - core)

    def near_chip(chip, core):
        return (chip ^ 1, core)

    def next_chip(chip, core):
        return (chip + 1 if chip % 2 else chip - 1, core)

    def far_over_next(chip, core):
        return (chip + 1 if core else chip - 1, 1 - core) if chip % 2 == core else None

    def far_over_near(chip, core):
        return (chip + 1 if core else chip - 1, 1 - core) if chip % 2 != core else None

    def chip_beyond(chip, core):
        return (chip + 2 if core else chip - 2, 1 - core)

    own, first, second, scale = unit_rows(query_raw, passage_raw)
    paired = (pairing[0][:, None] == jnp.arange(rows, dtype=jnp.int32)[None, :]).astype(jnp.float32)
    blank = jnp.zeros((rows, rows), jnp.float32)
    partner = jnp.block([[blank, paired], [paired.T, blank]])

    near = swapped(own, near_chip)
    next_halves = [swapped(half, next_chip) for half in (first, second)]
    mate = swapped(own, other_core)
    far_first = swapped(near, far_over_next)
    far_second = [swapped(half, far_over_near) for half in next_halves]
    near_mate = swapped(near, other_core)

    count = 2 * rows
    square = (count, count)
    *scores, mass, far_score, passed = score_call(
        early_kernel,
        "early_scores",
        count,
        [square] * 5,
        [partner, own, near, *next_halves],
        [next_halves[0]],
    )
    next_mate = [swapped(half, other_core) for half in (passed, next_halves[1])]
    far_score, mate_score = side_scores(own, mate, far_score, 0)
    far_score = far_scores(own, far_second[0], far_score, 0)
    far_score = far_scores(own, far_second[1], far_score, 1)
    far_score = far_scores(own, far_first, far_score, 0)
    near_mate_score, next_mate_score, recip, spread, losses = score_call(
        total_kernel,
        "totals",
        count,
        [square, square, (1, count), (SPREAD, count), (1, rows)],
        [far_score, mass, scores[0], partner, own, mate_score, near_mate, *next_mate],
    )

    mate_row = swapped(recip, other_core)
    chip_rows = jnp.concatenate([recip, mate_row], axis=0)
    near_rows = swapped(chip_rows, near_chip)
    next_rows = swapped(chip_rows, next_chip)
    far_row = swapped(spread, chip_beyond)

    near_score, next_score = scores[1:]
    part_sum, along = part_gradients(
        partner,
        [recip, mate_row, far_row, next_rows],
        [scores[0], mate_score, far_score, next_score, next_mate_score],
        [own, mate, far_first, *far_second, *next_halves, *next_mate],
    )
    query_grad, passage_grad = gradients(
        part_sum,
        along,
        scale,
        [recip, near_rows],
        [near_score, near_mate_score],
        [near, near_mate],
        query_raw,
        passage_raw,
    )
    return (losses.reshape(rows), query_grad, passage_grad)


def solution(mesh):
    in_specs = (P("dp", None), P("dp", None), P("dp", None))
    out_specs = (P("dp"), P("dp", None), P("dp", None))
    return jax.shard_map(
        per_device, mesh=mesh, in_specs=in_specs, out_specs=out_specs, check_vma=False
    )
```

```python
import functools

import jax
import jax.numpy as jnp
from jax import lax
from jax.experimental import pallas as pl
from jax.experimental.pallas import tpu as pltpu
from jax.sharding import PartitionSpec as P

INV_TEMP = 20.0
EPS = 1e-06
TILE = 896
VMEM = pl.BlockSpec(memory_space=pltpu.VMEM)
HBM = pl.BlockSpec(memory_space=pl.ANY)


def contract(left_rows, right_rows):
    return lax.dot_general(
        left_rows, right_rows, (((1,), (1,)), ((), ())), preferred_element_type=jnp.float32
    )


def exp_score(score):
    return jnp.exp(INV_TEMP * score - INV_TEMP)


def eye_of(count):
    down = lax.broadcasted_iota(jnp.int32, (count, count), 0)
    across = lax.broadcasted_iota(jnp.int32, (count, count), 1)
    return (down == across).astype(jnp.float32)


def unit_kernel(
    query_any, passage_any, own_ref, first_ref, second_ref, scale_ref, query_ref, passage_ref, sems
):
    copies = [
        pltpu.make_async_copy(query_any, query_ref, sems.at[0]),
        pltpu.make_async_copy(passage_any, passage_ref, sems.at[1]),
    ]
    for copy in copies:
        copy.start()
    for copy in copies:
        copy.wait()
    raw_rows = jnp.concatenate(
        [query_ref[...].astype(jnp.float32), passage_ref[...].astype(jnp.float32)], axis=0
    )
    scale_rows = lax.rsqrt(jnp.sum(raw_rows * raw_rows, axis=1, keepdims=True) + EPS)
    low_rows = (raw_rows * scale_rows).astype(jnp.bfloat16)
    width = first_ref.shape[1]
    own_ref[...] = low_rows
    first_ref[...] = low_rows[:, :width]
    second_ref[...] = low_rows[:, width:]
    scale_ref[...] = scale_rows


def unit_rows(query_raw, passage_raw):
    rows, width = query_raw.shape
    whole = jax.ShapeDtypeStruct((2 * rows, width), jnp.bfloat16)
    half = jax.ShapeDtypeStruct((2 * rows, width // 2), jnp.bfloat16)
    return pl.pallas_call(
        unit_kernel,
        in_specs=[HBM, HBM],
        out_specs=(VMEM, VMEM, VMEM, VMEM),
        out_shape=(whole, half, half, jax.ShapeDtypeStruct((2 * rows, 1), jnp.float32)),
        scratch_shapes=[
            pltpu.VMEM((rows, width), jnp.bfloat16),
            pltpu.VMEM((rows, width), jnp.bfloat16),
            pltpu.SemaphoreType.DMA((2,)),
        ],
        compiler_params=pltpu.CompilerParams(vmem_limit_bytes=121 * 2**19),
        cost_estimate=pl.CostEstimate(
            flops=6 * rows * width, bytes_accessed=8 * rows * width, transcendentals=0
        ),
        name="unit_rows",
    )(query_raw, passage_raw)


def score_call(body, name, count, outs, operands, passed=()):
    size = sum(operand.size for operand in operands)
    return pl.pallas_call(
        body,
        in_specs=[VMEM] * len(operands),
        out_specs=[VMEM] * (len(outs) + len(passed)),
        out_shape=[jax.ShapeDtypeStruct(shape, jnp.float32) for shape in outs]
        + [jax.ShapeDtypeStruct(value.shape, value.dtype) for value in passed],
        compiler_params=pltpu.CompilerParams(vmem_limit_bytes=16 * 2**20),
        cost_estimate=pl.CostEstimate(
            flops=2 * count * size, bytes_accessed=2 * size, transcendentals=count * count
        ),
        name=name,
    )(*operands)


def halves_score(own, first, second):
    width = first.shape[1]
    return contract(own[:, :width], first) + contract(own[:, width:], second)


def early_kernel(
    partner_ref, own_ref, near_ref, next_first, next_second, *outs
):
    *score_outs, mass_ref, blank_ref, passed_ref = outs
    partner = partner_ref[...]
    count = partner.shape[0]
    down = lax.broadcasted_iota(jnp.int32, (count, count), 0)
    keep = 1.0 - eye_of(count) - jnp.where(down >= count // 2, partner, 0.0)
    own = own_ref[...]
    scores = [
        contract(own, own),
        contract(own, near_ref[...]),
        halves_score(own, next_first[...], next_second[...]),
    ]
    mass = exp_score(scores[0]) * keep
    for score in scores[1:]:
        mass = mass + exp_score(score)
    for score, score_out in zip(scores, score_outs):
        score_out[...] = score
    mass_ref[...] = mass
    blank_ref[...] = jnp.zeros((count, count), jnp.float32)
    passed_ref[...] = next_first[...]


def far_kernel(place, own_ref, far_ref, sum_ref, score_ref):
    width = far_ref.shape[1]
    own = own_ref[:, place * width : (place + 1) * width]
    score_ref[...] = sum_ref[...] + contract(own, far_ref[...])


def far_scores(own, far, score_sum, place):
    count = own.shape[0]
    body = functools.partial(far_kernel, place)
    return score_call(body, "far_scores", count, [(count, count)], [own, far, score_sum])[0]


def side_kernel(place, sum_ref, own_ref, key_ref, sum_out, score_out):
    width = key_ref.shape[1]
    sum_out[...] = sum_ref[...]
    score_out[...] = contract(own_ref[:, place * width : (place + 1) * width], key_ref[...])


def side_scores(own, key, score_sum, place):
    count = own.shape[0]
    body = functools.partial(side_kernel, place)
    return score_call(body, "side_scores", count, [(count, count)] * 2, [score_sum, own, key])


def total_kernel(
    far_score_ref, mass_ref, score_ref, partner_ref, own_ref, own_mate_score, near_mate_ref, mate_first, mate_second,
    near_mate_out, next_mate_out, recip_ref, loss_ref,
):
    partner = partner_ref[...]
    own = own_ref[...]
    mass = mass_ref[...] + exp_score(far_score_ref[...])
    mass = mass + exp_score(own_mate_score[...])
    near_score = contract(own, near_mate_ref[...])
    near_mate_out[...] = near_score
    mass = mass + exp_score(near_score)
    next_score = halves_score(own, mate_first[...], mate_second[...])
    next_mate_out[...] = next_score
    mass = mass + exp_score(next_score)
    total_col = jnp.sum(mass, axis=1, keepdims=True)
    eye = eye_of(partner.shape[0])
    norm_row = jnp.sum((eye + partner) * total_col, axis=0, keepdims=True)
    recip_ref[...] = 1.0 / norm_row
    positive = jnp.sum(partner * score_ref[...], axis=0, keepdims=True)
    losses = jnp.log(norm_row) + INV_TEMP - INV_TEMP * positive
    loss_ref[...] = losses[:, : loss_ref.shape[1]]


def weigh(score, recip_col, recip_row):
    weight = exp_score(score) * (recip_col + recip_row)
    low = weight.astype(jnp.bfloat16)
    return low, low.astype(jnp.float32) * score


def column_of(row):
    return jnp.sum(eye_of(row.shape[1]) * row, axis=1, keepdims=True)


def part_kernel(
    partner_ref, own_row, mate_row, next_rows, own_score, mate_score, next_score, next_mate_score,
    own_ref, mate_ref, next_0, next_1, pair_0, pair_1, sum_ref, along_ref,
):
    partner = partner_ref[...]
    count = partner.shape[0]
    recip_row = own_row[...]
    recip_col = column_of(recip_row)
    score = own_score[...]
    weight = exp_score(score) * (recip_col + recip_row)
    weight = weight * (1.0 - eye_of(count)) * (1.0 - 0.5 * partner) - partner
    low = weight.astype(jnp.bfloat16)
    weights = [low]
    along = low.astype(jnp.float32) * score
    for score_ref, row in (
        (mate_score, mate_row[...]),
        (next_score, next_rows[0:1, :]),
        (next_mate_score, next_rows[1:2, :]),
    ):
        low, share = weigh(score_ref[...], recip_col, row)
        weights.append(low)
        along = along + share
    along_ref[...] = along
    weights = jnp.concatenate(weights, axis=1)
    half = next_0.shape[1]
    for start in range(0, own_ref.shape[1], TILE):
        whole = slice(start, start + TILE)
        columns = slice(start % half, start % half + TILE)
        next_ref, pair_ref = ((next_0, pair_0), (next_1, pair_1))[start // half]
        keys = [
            own_ref[:, whole],
            mate_ref[:, whole],
            next_ref[:, columns],
            pair_ref[:, columns],
        ]
        keys = jnp.concatenate(keys, axis=0)
        sum_ref[:, whole] = jnp.dot(weights, keys, preferred_element_type=jnp.float32)


def part_gradients(partner, rows, scores, keys):
    count = partner.shape[0]
    width = keys[0].shape[1]
    operands = [partner, *rows, *scores, *keys]
    return pl.pallas_call(
        part_kernel,
        in_specs=[VMEM] * len(operands),
        out_specs=(VMEM, VMEM),
        out_shape=(
            jax.ShapeDtypeStruct((count, width), jnp.float32),
            jax.ShapeDtypeStruct((count, count), jnp.float32),
        ),
        compiler_params=pltpu.CompilerParams(vmem_limit_bytes=24 * 2**20),
        cost_estimate=pl.CostEstimate(
            flops=8 * count * count * width,
            bytes_accessed=12 * count * width,
            transcendentals=4 * count * count,
        ),
        name="part_gradients",
    )(*operands)


def gradient_kernel(
    sum_ref, along_ref, scale_ref, own_row, near_rows, far_row, near_score, pair_score, far_score,
    near_ref, pair_ref, far_first, far_0, far_1, query_ref, passage_ref,
    query_out, passage_out, query_hold, passage_hold, sems,
):
    count = along_ref.shape[0]
    rows = count // 2
    recip_col = column_of(own_row[...])
    near_low, near_share = weigh(near_score[...], recip_col, near_rows[0:1, :])
    pair_low, pair_share = weigh(pair_score[...], recip_col, near_rows[1:2, :])
    far_low, far_share = weigh(far_score[...], recip_col, far_row[...])
    along = along_ref[...] + near_share + pair_share + far_share
    along = INV_TEMP * jnp.sum(along, axis=1, keepdims=True)
    weights = jnp.concatenate([near_low, pair_low, far_low], axis=1)
    half = far_0.shape[1]
    scale = scale_ref[...]
    copies = []
    for start in range(0, near_ref.shape[1], TILE):
        whole = slice(start, start + TILE)
        far_ref = (far_0, far_1)[start // half]
        far = far_first[:, whole] + far_ref[:, start % half : start % half + TILE]
        keys = jnp.concatenate([near_ref[:, whole], pair_ref[:, whole], far], axis=0)
        gradient = jnp.dot(weights, keys, preferred_element_type=jnp.float32) + sum_ref[:, whole]
        for part, raw_ref, hold, out in (
            (0, query_ref, query_hold, query_out),
            (1, passage_ref, passage_hold, passage_out),
        ):
            span = slice(part * rows, (part + 1) * rows)
            unit = raw_ref[:, whole].astype(jnp.float32) * scale[span]
            hold[:, whole] = (INV_TEMP * gradient[span] - unit * along[span]) * scale[span]
            copy = pltpu.make_async_copy(
                hold.at[:, whole], out.at[:, whole], sems.at[len(copies)]
            )
            copy.start()
            copies.append(copy)
    for copy in copies:
        copy.wait()


def gradients(part_sum, along, scale, rows, scores, keys, query_raw, passage_raw):
    count, width = part_sum.shape
    out = jax.ShapeDtypeStruct((count // 2, width), jnp.float32)
    operands = [part_sum, along, scale, *rows, *scores, *keys, query_raw, passage_raw]
    return pl.pallas_call(
        gradient_kernel,
        in_specs=[VMEM] * len(operands),
        out_specs=(HBM, HBM),
        out_shape=(out, out),
        scratch_shapes=[
            pltpu.VMEM((count // 2, width), jnp.float32),
            pltpu.VMEM((count // 2, width), jnp.float32),
            pltpu.SemaphoreType.DMA((2 * width // TILE,)),
        ],
        compiler_params=pltpu.CompilerParams(vmem_limit_bytes=24 * 2**20),
        cost_estimate=pl.CostEstimate(
            flops=6 * count * count * width,
            bytes_accessed=16 * count * width,
            transcendentals=3 * count * count,
        ),
        name="gradients",
    )(*operands)


def per_device(query_raw, passage_raw, pairing):
    size = lax.axis_size("dp")
    chips = size // 2
    rows = query_raw.shape[0]

    def swapped(value, partner_of):
        pairs = []
        for source in range(size):
            target = partner_of(source // 2, source % 2)
            if target is not None:
                pairs.append((source, (target[0] % chips) * 2 + target[1]))
        return lax.ppermute(value, "dp", pairs)

    def other_core(chip, core):
        return (chip, 1 - core)

    def near_chip(chip, core):
        return (chip ^ 1, core)

    def next_chip(chip, core):
        return (chip + 1 if chip % 2 else chip - 1, core)

    def far_over_next(chip, core):
        return (chip + 1 if core else chip - 1, 1 - core) if chip % 2 == core else None

    def far_over_near(chip, core):
        return (chip + 1 if core else chip - 1, 1 - core) if chip % 2 != core else None

    def chip_beyond(chip, core):
        return (chip + 2 if core else chip - 2, 1 - core)

    own, first, second, scale = unit_rows(query_raw, passage_raw)
    paired = (pairing[0][:, None] == jnp.arange(rows, dtype=jnp.int32)[None, :]).astype(jnp.float32)
    blank = jnp.zeros((rows, rows), jnp.float32)
    partner = jnp.block([[blank, paired], [paired.T, blank]])

    near = swapped(own, near_chip)
    next_halves = [swapped(half, next_chip) for half in (first, second)]
    mate = swapped(own, other_core)
    far_first = swapped(near, far_over_next)
    far_second = [swapped(half, far_over_near) for half in next_halves]
    near_mate = swapped(near, other_core)

    count = 2 * rows
    square = (count, count)
    *scores, mass, far_score, passed = score_call(
        early_kernel,
        "early_scores",
        count,
        [square] * 5,
        [partner, own, near, *next_halves],
        [next_halves[0]],
    )
    next_mate = [swapped(half, other_core) for half in (passed, next_halves[1])]
    far_score, mate_score = side_scores(own, mate, far_score, 0)
    far_score = far_scores(own, far_second[0], far_score, 0)
    far_score = far_scores(own, far_second[1], far_score, 1)
    far_score = far_scores(own, far_first, far_score, 0)
    near_mate_score, next_mate_score, recip, losses = score_call(
        total_kernel,
        "totals",
        count,
        [square, square, (1, count), (1, rows)],
        [far_score, mass, scores[0], partner, own, mate_score, near_mate, *next_mate],
    )

    mate_row = swapped(recip, other_core)
    chip_rows = jnp.concatenate([recip, mate_row], axis=0)
    near_rows = swapped(chip_rows, near_chip)
    next_rows = swapped(chip_rows, next_chip)
    far_row = swapped(recip, chip_beyond)

    near_score, next_score = scores[1:]
    part_sum, along = part_gradients(
        partner,
        [recip, mate_row, next_rows],
        [scores[0], mate_score, next_score, next_mate_score],
        [own, mate, *next_halves, *next_mate],
    )
    query_grad, passage_grad = gradients(
        part_sum,
        along,
        scale,
        [recip, near_rows, far_row],
        [near_score, near_mate_score, far_score],
        [near, near_mate, far_first, *far_second],
        query_raw,
        passage_raw,
    )
    return (losses.reshape(rows), query_grad, passage_grad)


def solution(mesh):
    in_specs = (P("dp", None), P("dp", None), P("dp", None))
    out_specs = (P("dp"), P("dp", None), P("dp", None))
    return jax.shard_map(
        per_device, mesh=mesh, in_specs=in_specs, out_specs=out_specs, check_vma=False
    )
```

```python
import functools

import jax
import jax.numpy as jnp
from jax import lax
from jax.experimental import pallas as pl
from jax.experimental.pallas import tpu as pltpu
from jax.sharding import PartitionSpec as P

INV_TEMP = 20.0
EPS = 1e-06
TILE = 896
SPREAD = 8
CHUNK = 48
VMEM = pl.BlockSpec(memory_space=pltpu.VMEM)
HBM = pl.BlockSpec(memory_space=pl.ANY)


def contract(left_rows, right_rows):
    return lax.dot_general(
        left_rows, right_rows, (((1,), (1,)), ((), ())), preferred_element_type=jnp.float32
    )


def exp_score(score):
    return jnp.exp(INV_TEMP * score - INV_TEMP)


def eye_of(count):
    down = lax.broadcasted_iota(jnp.int32, (count, count), 0)
    across = lax.broadcasted_iota(jnp.int32, (count, count), 1)
    return (down == across).astype(jnp.float32)


def unit_kernel(
    query_any, passage_any, own_out, first_out, second_out, scale_ref,
    query_ref, passage_ref, hold_ref, in_sems, out_sems,
):
    reads = [
        pltpu.make_async_copy(query_any, query_ref, in_sems.at[0]),
        pltpu.make_async_copy(passage_any, passage_ref, in_sems.at[1]),
    ]
    for copy in reads:
        copy.start()
    for copy in reads:
        copy.wait()
    raw_rows = jnp.concatenate(
        [query_ref[...].astype(jnp.float32), passage_ref[...].astype(jnp.float32)], axis=0
    )
    count, width = hold_ref.shape
    half = width // 2
    writes = []
    for start in range(0, count, CHUNK):
        rows = slice(start, start + CHUNK)
        chunk = raw_rows[rows]
        scale_rows = lax.rsqrt(jnp.sum(chunk * chunk, axis=1, keepdims=True) + EPS)
        hold_ref[rows, :] = (chunk * scale_rows).astype(jnp.bfloat16)
        scale_ref[rows, :] = scale_rows
        for columns, out in (
            (slice(0, width), own_out),
            (slice(0, half), first_out),
            (slice(half, width), second_out),
        ):
            copy = pltpu.make_async_copy(
                hold_ref.at[rows, columns], out.at[rows, :], out_sems.at[len(writes)]
            )
            copy.start()
            writes.append(copy)
    for copy in writes:
        copy.wait()


def unit_rows(query_raw, passage_raw):
    rows, width = query_raw.shape
    whole = jax.ShapeDtypeStruct((2 * rows, width), jnp.bfloat16)
    half = jax.ShapeDtypeStruct((2 * rows, width // 2), jnp.bfloat16)
    return pl.pallas_call(
        unit_kernel,
        in_specs=[HBM, HBM],
        out_specs=(HBM, HBM, HBM, VMEM),
        out_shape=(whole, half, half, jax.ShapeDtypeStruct((2 * rows, 1), jnp.float32)),
        scratch_shapes=[
            pltpu.VMEM((rows, width), jnp.bfloat16),
            pltpu.VMEM((rows, width), jnp.bfloat16),
            pltpu.VMEM((2 * rows, width), jnp.bfloat16),
            pltpu.SemaphoreType.DMA((2,)),
            pltpu.SemaphoreType.DMA((3 * 2 * rows // CHUNK,)),
        ],
        compiler_params=pltpu.CompilerParams(vmem_limit_bytes=121 * 2**19),
        cost_estimate=pl.CostEstimate(
            flops=6 * rows * width, bytes_accessed=8 * rows * width, transcendentals=0
        ),
        name="unit_rows",
    )(query_raw, passage_raw)


def score_call(body, name, count, outs, operands, passed=()):
    size = sum(operand.size for operand in operands)
    return pl.pallas_call(
        body,
        in_specs=[VMEM] * len(operands),
        out_specs=[VMEM] * (len(outs) + len(passed)),
        out_shape=[jax.ShapeDtypeStruct(shape, jnp.float32) for shape in outs]
        + [jax.ShapeDtypeStruct(value.shape, value.dtype) for value in passed],
        compiler_params=pltpu.CompilerParams(vmem_limit_bytes=16 * 2**20),
        cost_estimate=pl.CostEstimate(
            flops=2 * count * size, bytes_accessed=2 * size, transcendentals=count * count
        ),
        name=name,
    )(*operands)


def halves_score(own, first, second):
    width = first.shape[1]
    return contract(own[:, :width], first) + contract(own[:, width:], second)


def early_kernel(
    partner_ref, own_ref, near_ref, next_first, next_second, *outs
):
    *score_outs, mass_ref, blank_ref, passed_ref = outs
    partner = partner_ref[...]
    count = partner.shape[0]
    down = lax.broadcasted_iota(jnp.int32, (count, count), 0)
    keep = 1.0 - eye_of(count) - jnp.where(down >= count // 2, partner, 0.0)
    own = own_ref[...]
    scores = [
        contract(own, own),
        contract(own, near_ref[...]),
        halves_score(own, next_first[...], next_second[...]),
    ]
    mass = exp_score(scores[0]) * keep
    for score in scores[1:]:
        mass = mass + exp_score(score)
    for score, score_out in zip(scores, score_outs):
        score_out[...] = score
    mass_ref[...] = mass
    blank_ref[...] = jnp.zeros((count, count), jnp.float32)
    passed_ref[...] = next_first[...]


def far_kernel(place, own_ref, far_ref, sum_ref, score_ref):
    width = far_ref.shape[1]
    own = own_ref[:, place * width : (place + 1) * width]
    score_ref[...] = sum_ref[...] + contract(own, far_ref[...])


def far_scores(own, far, score_sum, place):
    count = own.shape[0]
    body = functools.partial(far_kernel, place)
    return score_call(body, "far_scores", count, [(count, count)], [own, far, score_sum])[0]


def side_kernel(place, sum_ref, own_ref, key_ref, sum_out, score_out):
    width = key_ref.shape[1]
    sum_out[...] = sum_ref[...]
    score_out[...] = contract(own_ref[:, place * width : (place + 1) * width], key_ref[...])


def side_scores(own, key, score_sum, place):
    count = own.shape[0]
    body = functools.partial(side_kernel, place)
    return score_call(body, "side_scores", count, [(count, count)] * 2, [score_sum, own, key])


def total_kernel(
    far_score_ref, mass_ref, score_ref, partner_ref, own_ref, own_mate_score, near_mate_ref, mate_first, mate_second,
    near_mate_out, next_mate_out, recip_ref, spread_ref, loss_ref,
):
    partner = partner_ref[...]
    own = own_ref[...]
    mass = mass_ref[...] + exp_score(far_score_ref[...])
    mass = mass + exp_score(own_mate_score[...])
    near_score = contract(own, near_mate_ref[...])
    near_mate_out[...] = near_score
    mass = mass + exp_score(near_score)
    next_score = halves_score(own, mate_first[...], mate_second[...])
    next_mate_out[...] = next_score
    mass = mass + exp_score(next_score)
    total_col = jnp.sum(mass, axis=1, keepdims=True)
    eye = eye_of(partner.shape[0])
    norm_row = jnp.sum((eye + partner) * total_col, axis=0, keepdims=True)
    recip_ref[...] = 1.0 / norm_row
    spread_ref[...] = jnp.broadcast_to(1.0 / norm_row, spread_ref.shape)
    positive = jnp.sum(partner * score_ref[...], axis=0, keepdims=True)
    losses = jnp.log(norm_row) + INV_TEMP - INV_TEMP * positive
    loss_ref[...] = losses[:, : loss_ref.shape[1]]


def weigh(score, recip_col, recip_row):
    weight = exp_score(score) * (recip_col + recip_row)
    low = weight.astype(jnp.bfloat16)
    return low, low.astype(jnp.float32) * score


def column_of(row):
    return jnp.sum(eye_of(row.shape[1]) * row, axis=1, keepdims=True)


def part_kernel(
    partner_ref, own_row, mate_row, even_row, next_rows, own_score, mate_score, next_score, next_mate_score,
    own_ref, mate_ref, next_0, next_1, pair_0, pair_1, sum_ref, along_ref, passed_ref,
):
    partner = partner_ref[...]
    count = partner.shape[0]
    recip_row = own_row[...]
    recip_col = column_of(recip_row)
    score = own_score[...]
    weight = exp_score(score) * (recip_col + recip_row)
    weight = weight * (1.0 - eye_of(count)) * (1.0 - 0.5 * partner) - partner
    low = weight.astype(jnp.bfloat16)
    weights = [low]
    along = low.astype(jnp.float32) * score
    for score_ref, row in (
        (mate_score, mate_row[...]),
        (next_score, next_rows[0:1, :]),
        (next_mate_score, next_rows[1:2, :]),
    ):
        low, share = weigh(score_ref[...], recip_col, row)
        weights.append(low)
        along = along + share
    along_ref[...] = along
    passed_ref[...] = even_row[0:1, :]
    weights = jnp.concatenate(weights, axis=1)
    half = next_0.shape[1]
    for start in range(0, own_ref.shape[1], TILE):
        whole = slice(start, start + TILE)
        columns = slice(start % half, start % half + TILE)
        next_ref, pair_ref = ((next_0, pair_0), (next_1, pair_1))[start // half]
        keys = [
            own_ref[:, whole],
            mate_ref[:, whole],
            next_ref[:, columns],
            pair_ref[:, columns],
        ]
        keys = jnp.concatenate(keys, axis=0)
        sum_ref[:, whole] = jnp.dot(weights, keys, preferred_element_type=jnp.float32)


def part_gradients(partner, rows, scores, keys):
    count = partner.shape[0]
    width = keys[0].shape[1]
    operands = [partner, *rows, *scores, *keys]
    return pl.pallas_call(
        part_kernel,
        in_specs=[VMEM] * len(operands),
        out_specs=(VMEM, VMEM, VMEM),
        out_shape=(
            jax.ShapeDtypeStruct((count, width), jnp.float32),
            jax.ShapeDtypeStruct((count, count), jnp.float32),
            jax.ShapeDtypeStruct((1, count), jnp.float32),
        ),
        compiler_params=pltpu.CompilerParams(vmem_limit_bytes=24 * 2**20),
        cost_estimate=pl.CostEstimate(
            flops=8 * count * count * width,
            bytes_accessed=12 * count * width,
            transcendentals=4 * count * count,
        ),
        name="part_gradients",
    )(*operands)


def gradient_kernel(
    sum_ref, along_ref, scale_ref, own_row, near_rows, even_row, odd_row, near_score, pair_score, far_score,
    near_ref, pair_ref, far_first, far_0, far_1, query_ref, passage_ref,
    query_out, passage_out, query_hold, passage_hold, sems,
):
    count = along_ref.shape[0]
    rows = count // 2
    recip_col = column_of(own_row[...])
    near_low, near_share = weigh(near_score[...], recip_col, near_rows[0:1, :])
    pair_low, pair_share = weigh(pair_score[...], recip_col, near_rows[1:2, :])
    far_low, far_share = weigh(far_score[...], recip_col, even_row[...] + odd_row[...])
    along = along_ref[...] + near_share + pair_share + far_share
    along = INV_TEMP * jnp.sum(along, axis=1, keepdims=True)
    weights = jnp.concatenate([near_low, pair_low, far_low], axis=1)
    half = far_0.shape[1]
    scale = scale_ref[...]
    copies = []
    for start in range(0, near_ref.shape[1], TILE):
        whole = slice(start, start + TILE)
        far_ref = (far_0, far_1)[start // half]
        far = far_first[:, whole] + far_ref[:, start % half : start % half + TILE]
        keys = jnp.concatenate([near_ref[:, whole], pair_ref[:, whole], far], axis=0)
        gradient = jnp.dot(weights, keys, preferred_element_type=jnp.float32) + sum_ref[:, whole]
        for part, raw_ref, hold, out in (
            (0, query_ref, query_hold, query_out),
            (1, passage_ref, passage_hold, passage_out),
        ):
            span = slice(part * rows, (part + 1) * rows)
            unit = raw_ref[:, whole].astype(jnp.float32) * scale[span]
            hold[:, whole] = (INV_TEMP * gradient[span] - unit * along[span]) * scale[span]
            copy = pltpu.make_async_copy(
                hold.at[:, whole], out.at[:, whole], sems.at[len(copies)]
            )
            copy.start()
            copies.append(copy)
    for copy in copies:
        copy.wait()


def gradients(part_sum, along, scale, rows, scores, keys, query_raw, passage_raw):
    count, width = part_sum.shape
    out = jax.ShapeDtypeStruct((count // 2, width), jnp.float32)
    operands = [part_sum, along, scale, *rows, *scores, *keys, query_raw, passage_raw]
    return pl.pallas_call(
        gradient_kernel,
        in_specs=[VMEM] * len(operands),
        out_specs=(HBM, HBM),
        out_shape=(out, out),
        scratch_shapes=[
            pltpu.VMEM((count // 2, width), jnp.float32),
            pltpu.VMEM((count // 2, width), jnp.float32),
            pltpu.SemaphoreType.DMA((2 * width // TILE,)),
        ],
        compiler_params=pltpu.CompilerParams(vmem_limit_bytes=24 * 2**20),
        cost_estimate=pl.CostEstimate(
            flops=6 * count * count * width,
            bytes_accessed=16 * count * width,
            transcendentals=3 * count * count,
        ),
        name="gradients",
    )(*operands)


def per_device(query_raw, passage_raw, pairing):
    size = lax.axis_size("dp")
    chips = size // 2
    rows = query_raw.shape[0]

    def swapped(value, partner_of):
        pairs = []
        for source in range(size):
            target = partner_of(source // 2, source % 2)
            if target is not None:
                pairs.append((source, (target[0] % chips) * 2 + target[1]))
        return lax.ppermute(value, "dp", pairs)

    def other_core(chip, core):
        return (chip, 1 - core)

    def near_chip(chip, core):
        return (chip ^ 1, core)

    def next_chip(chip, core):
        return (chip + 1 if chip % 2 else chip - 1, core)

    def far_over_next(chip, core):
        return (chip + 1 if core else chip - 1, 1 - core) if chip % 2 == core else None

    def far_over_near(chip, core):
        return (chip + 1 if core else chip - 1, 1 - core) if chip % 2 != core else None

    def beyond_of(parity, chip, core):
        return (chip + 2 if core else chip - 2, 1 - core) if chip % 2 == parity else None

    own, first, second, scale = unit_rows(query_raw, passage_raw)
    paired = (pairing[0][:, None] == jnp.arange(rows, dtype=jnp.int32)[None, :]).astype(jnp.float32)
    blank = jnp.zeros((rows, rows), jnp.float32)
    partner = jnp.block([[blank, paired], [paired.T, blank]])

    near = swapped(own, near_chip)
    next_halves = [swapped(half, next_chip) for half in (first, second)]
    mate = swapped(own, other_core)
    far_first = swapped(near, far_over_next)
    far_second = [swapped(half, far_over_near) for half in next_halves]
    near_mate = swapped(near, other_core)

    count = 2 * rows
    square = (count, count)
    *scores, mass, far_score, passed = score_call(
        early_kernel,
        "early_scores",
        count,
        [square] * 5,
        [partner, own, near, *next_halves],
        [next_halves[0]],
    )
    next_mate = [swapped(half, other_core) for half in (passed, next_halves[1])]
    far_score = far_scores(own, far_second[0], far_score, 0)
    far_score, mate_score = side_scores(own, mate, far_score, 0)
    far_score = far_scores(own, far_second[1], far_score, 1)
    far_score = far_scores(own, far_first, far_score, 0)
    near_mate_score, next_mate_score, recip, spread, losses = score_call(
        total_kernel,
        "totals",
        count,
        [square, square, (1, count), (SPREAD, count), (1, rows)],
        [far_score, mass, scores[0], partner, own, mate_score, near_mate, *next_mate],
    )

    mate_row = swapped(recip, other_core)
    chip_rows = jnp.concatenate([recip, mate_row], axis=0)
    near_rows = swapped(chip_rows, near_chip)
    next_rows = swapped(chip_rows, next_chip)
    even_row = swapped(spread, functools.partial(beyond_of, 0))
    odd_row = swapped(recip, functools.partial(beyond_of, 1))

    near_score, next_score = scores[1:]
    part_sum, along, even_row = part_gradients(
        partner,
        [recip, mate_row, even_row, next_rows],
        [scores[0], mate_score, next_score, next_mate_score],
        [own, mate, *next_halves, *next_mate],
    )
    query_grad, passage_grad = gradients(
        part_sum,
        along,
        scale,
        [recip, near_rows, even_row, odd_row],
        [near_score, near_mate_score, far_score],
        [near, near_mate, far_first, *far_second],
        query_raw,
        passage_raw,
    )
    return (losses.reshape(rows), query_grad, passage_grad)


def solution(mesh):
    in_specs = (P("dp", None), P("dp", None), P("dp", None))
    out_specs = (P("dp"), P("dp", None), P("dp", None))
    return jax.shard_map(
        per_device, mesh=mesh, in_specs=in_specs, out_specs=out_specs, check_vma=False
    )
```

```python
import functools

import jax
import jax.numpy as jnp
from jax import lax
from jax.experimental import pallas as pl
from jax.experimental.pallas import tpu as pltpu
from jax.sharding import PartitionSpec as P

INV_TEMP = 20.0
EPS = 1e-06
TILE = 896
SPREAD = 8
VMEM = pl.BlockSpec(memory_space=pltpu.VMEM)
HBM = pl.BlockSpec(memory_space=pl.ANY)


def contract(left_rows, right_rows):
    return lax.dot_general(
        left_rows, right_rows, (((1,), (1,)), ((), ())), preferred_element_type=jnp.float32
    )


def exp_score(score):
    return jnp.exp(INV_TEMP * score - INV_TEMP)


def eye_of(count):
    down = lax.broadcasted_iota(jnp.int32, (count, count), 0)
    across = lax.broadcasted_iota(jnp.int32, (count, count), 1)
    return (down == across).astype(jnp.float32)


def unit_kernel(
    query_any, passage_any, own_ref, first_ref, second_ref, scale_ref, query_ref, passage_ref, sems
):
    copies = [
        pltpu.make_async_copy(query_any, query_ref, sems.at[0]),
        pltpu.make_async_copy(passage_any, passage_ref, sems.at[1]),
    ]
    for copy in copies:
        copy.start()
    for copy in copies:
        copy.wait()
    raw_rows = jnp.concatenate(
        [query_ref[...].astype(jnp.float32), passage_ref[...].astype(jnp.float32)], axis=0
    )
    scale_rows = lax.rsqrt(jnp.sum(raw_rows * raw_rows, axis=1, keepdims=True) + EPS)
    low_rows = (raw_rows * scale_rows).astype(jnp.bfloat16)
    width = first_ref.shape[1]
    own_ref[...] = low_rows
    first_ref[...] = low_rows[:, :width]
    second_ref[...] = low_rows[:, width:]
    scale_ref[...] = scale_rows


def unit_rows(query_raw, passage_raw):
    rows, width = query_raw.shape
    whole = jax.ShapeDtypeStruct((2 * rows, width), jnp.bfloat16)
    half = jax.ShapeDtypeStruct((2 * rows, width // 2), jnp.bfloat16)
    return pl.pallas_call(
        unit_kernel,
        in_specs=[HBM, HBM],
        out_specs=(VMEM, VMEM, VMEM, VMEM),
        out_shape=(whole, half, half, jax.ShapeDtypeStruct((2 * rows, 1), jnp.float32)),
        scratch_shapes=[
            pltpu.VMEM((rows, width), jnp.bfloat16),
            pltpu.VMEM((rows, width), jnp.bfloat16),
            pltpu.SemaphoreType.DMA((2,)),
        ],
        compiler_params=pltpu.CompilerParams(vmem_limit_bytes=121 * 2**19),
        cost_estimate=pl.CostEstimate(
            flops=6 * rows * width, bytes_accessed=8 * rows * width, transcendentals=0
        ),
        name="unit_rows",
    )(query_raw, passage_raw)


def score_call(body, name, count, outs, operands, passed=()):
    size = sum(operand.size for operand in operands)
    return pl.pallas_call(
        body,
        in_specs=[VMEM] * len(operands),
        out_specs=[VMEM] * (len(outs) + len(passed)),
        out_shape=[jax.ShapeDtypeStruct(shape, jnp.float32) for shape in outs]
        + [jax.ShapeDtypeStruct(value.shape, value.dtype) for value in passed],
        compiler_params=pltpu.CompilerParams(vmem_limit_bytes=16 * 2**20),
        cost_estimate=pl.CostEstimate(
            flops=2 * count * size, bytes_accessed=2 * size, transcendentals=count * count
        ),
        name=name,
    )(*operands)


def halves_score(own, first, second):
    width = first.shape[1]
    return contract(own[:, :width], first) + contract(own[:, width:], second)


def early_kernel(
    partner_ref, own_ref, near_ref, next_first, next_second, *outs
):
    *score_outs, mass_ref, blank_ref, passed_ref = outs
    partner = partner_ref[...]
    count = partner.shape[0]
    down = lax.broadcasted_iota(jnp.int32, (count, count), 0)
    keep = 1.0 - eye_of(count) - jnp.where(down >= count // 2, partner, 0.0)
    own = own_ref[...]
    scores = [
        contract(own, own),
        contract(own, near_ref[...]),
        halves_score(own, next_first[...], next_second[...]),
    ]
    mass = exp_score(scores[0]) * keep
    for score in scores[1:]:
        mass = mass + exp_score(score)
    for score, score_out in zip(scores, score_outs):
        score_out[...] = score
    mass_ref[...] = mass
    blank_ref[...] = jnp.zeros((count, count), jnp.float32)
    passed_ref[...] = next_first[...]


def far_kernel(place, own_ref, far_ref, sum_ref, score_ref):
    width = far_ref.shape[1]
    own = own_ref[:, place * width : (place + 1) * width]
    score_ref[...] = sum_ref[...] + contract(own, far_ref[...])


def far_scores(own, far, score_sum, place):
    count = own.shape[0]
    body = functools.partial(far_kernel, place)
    return score_call(body, "far_scores", count, [(count, count)], [own, far, score_sum])[0]


def side_kernel(place, sum_ref, own_ref, key_ref, sum_out, score_out):
    width = key_ref.shape[1]
    sum_out[...] = sum_ref[...]
    score_out[...] = contract(own_ref[:, place * width : (place + 1) * width], key_ref[...])


def side_scores(own, key, score_sum, place):
    count = own.shape[0]
    body = functools.partial(side_kernel, place)
    return score_call(body, "side_scores", count, [(count, count)] * 2, [score_sum, own, key])


def total_kernel(
    far_score_ref, mass_ref, score_ref, partner_ref, own_ref, own_mate_score, near_mate_ref, mate_first, mate_second,
    near_mate_out, next_mate_out, recip_ref, spread_ref, loss_ref,
):
    partner = partner_ref[...]
    own = own_ref[...]
    mass = mass_ref[...] + exp_score(far_score_ref[...])
    mass = mass + exp_score(own_mate_score[...])
    near_score = contract(own, near_mate_ref[...])
    near_mate_out[...] = near_score
    mass = mass + exp_score(near_score)
    next_score = halves_score(own, mate_first[...], mate_second[...])
    next_mate_out[...] = next_score
    mass = mass + exp_score(next_score)
    total_col = jnp.sum(mass, axis=1, keepdims=True)
    eye = eye_of(partner.shape[0])
    norm_row = jnp.sum((eye + partner) * total_col, axis=0, keepdims=True)
    recip_ref[...] = 1.0 / norm_row
    spread_ref[...] = jnp.broadcast_to(1.0 / norm_row, spread_ref.shape)
    positive = jnp.sum(partner * score_ref[...], axis=0, keepdims=True)
    losses = jnp.log(norm_row) + INV_TEMP - INV_TEMP * positive
    loss_ref[...] = losses[:, : loss_ref.shape[1]]


def weigh(score, recip_col, recip_row):
    weight = exp_score(score) * (recip_col + recip_row)
    low = weight.astype(jnp.bfloat16)
    return low, low.astype(jnp.float32) * score


def column_of(row):
    return jnp.sum(eye_of(row.shape[1]) * row, axis=1, keepdims=True)


def part_kernel(
    partner_ref, own_row, mate_row, even_row, near_rows, own_score, mate_score, near_score, pair_score,
    own_ref, mate_ref, near_ref, pair_ref, sum_ref, along_ref, passed_ref,
):
    partner = partner_ref[...]
    count = partner.shape[0]
    recip_row = own_row[...]
    recip_col = column_of(recip_row)
    score = own_score[...]
    weight = exp_score(score) * (recip_col + recip_row)
    weight = weight * (1.0 - eye_of(count)) * (1.0 - 0.5 * partner) - partner
    low = weight.astype(jnp.bfloat16)
    weights = [low]
    along = low.astype(jnp.float32) * score
    for score_ref, row in (
        (mate_score, mate_row[...]),
        (near_score, near_rows[0:1, :]),
        (pair_score, near_rows[1:2, :]),
    ):
        low, share = weigh(score_ref[...], recip_col, row)
        weights.append(low)
        along = along + share
    along_ref[...] = along
    passed_ref[...] = even_row[0:1, :]
    weights = jnp.concatenate(weights, axis=1)
    for start in range(0, own_ref.shape[1], TILE):
        whole = slice(start, start + TILE)
        keys = [own_ref[:, whole], mate_ref[:, whole], near_ref[:, whole], pair_ref[:, whole]]
        keys = jnp.concatenate(keys, axis=0)
        sum_ref[:, whole] = jnp.dot(weights, keys, preferred_element_type=jnp.float32)


def part_gradients(partner, rows, scores, keys):
    count = partner.shape[0]
    width = keys[0].shape[1]
    operands = [partner, *rows, *scores, *keys]
    return pl.pallas_call(
        part_kernel,
        in_specs=[VMEM] * len(operands),
        out_specs=(VMEM, VMEM, VMEM),
        out_shape=(
            jax.ShapeDtypeStruct((count, width), jnp.float32),
            jax.ShapeDtypeStruct((count, count), jnp.float32),
            jax.ShapeDtypeStruct((1, count), jnp.float32),
        ),
        compiler_params=pltpu.CompilerParams(vmem_limit_bytes=24 * 2**20),
        cost_estimate=pl.CostEstimate(
            flops=8 * count * count * width,
            bytes_accessed=12 * count * width,
            transcendentals=4 * count * count,
        ),
        name="part_gradients",
    )(*operands)


def gradient_kernel(
    sum_ref, along_ref, scale_ref, own_row, next_rows, even_row, odd_row, next_score, pair_score, far_score,
    next_0, next_1, pair_0, pair_1, far_first, far_0, far_1, query_ref, passage_ref,
    query_out, passage_out, query_hold, passage_hold, sems,
):
    count = along_ref.shape[0]
    rows = count // 2
    recip_col = column_of(own_row[...])
    next_low, next_share = weigh(next_score[...], recip_col, next_rows[0:1, :])
    pair_low, pair_share = weigh(pair_score[...], recip_col, next_rows[1:2, :])
    far_low, far_share = weigh(far_score[...], recip_col, even_row[...] + odd_row[...])
    along = along_ref[...] + next_share + pair_share + far_share
    along = INV_TEMP * jnp.sum(along, axis=1, keepdims=True)
    weights = jnp.concatenate([next_low, pair_low, far_low], axis=1)
    half = far_0.shape[1]
    scale = scale_ref[...]
    copies = []
    for start in range(0, far_first.shape[1], TILE):
        whole = slice(start, start + TILE)
        columns = slice(start % half, start % half + TILE)
        next_ref, pair_ref, far_ref = ((next_0, pair_0, far_0), (next_1, pair_1, far_1))[start // half]
        far = far_first[:, whole] + far_ref[:, columns]
        keys = jnp.concatenate([next_ref[:, columns], pair_ref[:, columns], far], axis=0)
        gradient = jnp.dot(weights, keys, preferred_element_type=jnp.float32) + sum_ref[:, whole]
        for part, raw_ref, hold, out in (
            (0, query_ref, query_hold, query_out),
            (1, passage_ref, passage_hold, passage_out),
        ):
            span = slice(part * rows, (part + 1) * rows)
            unit = raw_ref[:, whole].astype(jnp.float32) * scale[span]
            hold[:, whole] = (INV_TEMP * gradient[span] - unit * along[span]) * scale[span]
            copy = pltpu.make_async_copy(
                hold.at[:, whole], out.at[:, whole], sems.at[len(copies)]
            )
            copy.start()
            copies.append(copy)
    for copy in copies:
        copy.wait()


def gradients(part_sum, along, scale, rows, scores, keys, query_raw, passage_raw):
    count, width = part_sum.shape
    out = jax.ShapeDtypeStruct((count // 2, width), jnp.float32)
    operands = [part_sum, along, scale, *rows, *scores, *keys, query_raw, passage_raw]
    return pl.pallas_call(
        gradient_kernel,
        in_specs=[VMEM] * len(operands),
        out_specs=(HBM, HBM),
        out_shape=(out, out),
        scratch_shapes=[
            pltpu.VMEM((count // 2, width), jnp.float32),
            pltpu.VMEM((count // 2, width), jnp.float32),
            pltpu.SemaphoreType.DMA((2 * width // TILE,)),
        ],
        compiler_params=pltpu.CompilerParams(vmem_limit_bytes=24 * 2**20),
        cost_estimate=pl.CostEstimate(
            flops=6 * count * count * width,
            bytes_accessed=16 * count * width,
            transcendentals=3 * count * count,
        ),
        name="gradients",
    )(*operands)


def per_device(query_raw, passage_raw, pairing):
    size = lax.axis_size("dp")
    chips = size // 2
    rows = query_raw.shape[0]

    def swapped(value, partner_of):
        pairs = []
        for source in range(size):
            target = partner_of(source // 2, source % 2)
            if target is not None:
                pairs.append((source, (target[0] % chips) * 2 + target[1]))
        return lax.ppermute(value, "dp", pairs)

    def other_core(chip, core):
        return (chip, 1 - core)

    def near_chip(chip, core):
        return (chip ^ 1, core)

    def next_chip(chip, core):
        return (chip + 1 if chip % 2 else chip - 1, core)

    def far_over_next(chip, core):
        return (chip + 1 if core else chip - 1, 1 - core) if chip % 2 == core else None

    def far_over_near(chip, core):
        return (chip + 1 if core else chip - 1, 1 - core) if chip % 2 != core else None

    def beyond_of(parity, chip, core):
        return (chip + 2 if core else chip - 2, 1 - core) if chip % 2 == parity else None

    own, first, second, scale = unit_rows(query_raw, passage_raw)
    paired = (pairing[0][:, None] == jnp.arange(rows, dtype=jnp.int32)[None, :]).astype(jnp.float32)
    blank = jnp.zeros((rows, rows), jnp.float32)
    partner = jnp.block([[blank, paired], [paired.T, blank]])

    near = swapped(own, near_chip)
    next_halves = [swapped(half, next_chip) for half in (first, second)]
    mate = swapped(own, other_core)
    far_first = swapped(near, far_over_next)
    far_second = [swapped(half, far_over_near) for half in next_halves]
    near_mate = swapped(near, other_core)

    count = 2 * rows
    square = (count, count)
    *scores, mass, far_score, passed = score_call(
        early_kernel,
        "early_scores",
        count,
        [square] * 5,
        [partner, own, near, *next_halves],
        [next_halves[0]],
    )
    next_mate = [swapped(half, other_core) for half in (passed, next_halves[1])]
    far_score = far_scores(own, far_second[0], far_score, 0)
    far_score, mate_score = side_scores(own, mate, far_score, 0)
    far_score = far_scores(own, far_second[1], far_score, 1)
    far_score = far_scores(own, far_first, far_score, 0)
    near_mate_score, next_mate_score, recip, spread, losses = score_call(
        total_kernel,
        "totals",
        count,
        [square, square, (1, count), (SPREAD, count), (1, rows)],
        [far_score, mass, scores[0], partner, own, mate_score, near_mate, *next_mate],
    )

    mate_row = swapped(recip, other_core)
    chip_rows = jnp.concatenate([recip, mate_row], axis=0)
    near_rows = swapped(chip_rows, near_chip)
    next_rows = swapped(chip_rows, next_chip)
    even_row = swapped(spread, functools.partial(beyond_of, 0))
    odd_row = swapped(recip, functools.partial(beyond_of, 1))

    near_score, next_score = scores[1:]
    part_sum, along, even_row = part_gradients(
        partner,
        [recip, mate_row, even_row, near_rows],
        [scores[0], mate_score, near_score, near_mate_score],
        [own, mate, near, near_mate],
    )
    query_grad, passage_grad = gradients(
        part_sum,
        along,
        scale,
        [recip, next_rows, even_row, odd_row],
        [next_score, next_mate_score, far_score],
        [*next_halves, *next_mate, far_first, *far_second],
        query_raw,
        passage_raw,
    )
    return (losses.reshape(rows), query_grad, passage_grad)


def solution(mesh):
    in_specs = (P("dp", None), P("dp", None), P("dp", None))
    out_specs = (P("dp"), P("dp", None), P("dp", None))
    return jax.shard_map(
        per_device, mesh=mesh, in_specs=in_specs, out_specs=out_specs, check_vma=False
    )
```

```python
import functools

import jax
import jax.numpy as jnp
from jax import lax
from jax.experimental import pallas as pl
from jax.experimental.pallas import tpu as pltpu
from jax.sharding import PartitionSpec as P

INV_TEMP = 20.0
EPS = 1e-06
TILE = 896
SPREAD = 8
VMEM = pl.BlockSpec(memory_space=pltpu.VMEM)
HBM = pl.BlockSpec(memory_space=pl.ANY)


def contract(left_rows, right_rows):
    return lax.dot_general(
        left_rows, right_rows, (((1,), (1,)), ((), ())), preferred_element_type=jnp.float32
    )


def exp_score(score):
    return jnp.exp(INV_TEMP * score - INV_TEMP)


def eye_of(count):
    down = lax.broadcasted_iota(jnp.int32, (count, count), 0)
    across = lax.broadcasted_iota(jnp.int32, (count, count), 1)
    return (down == across).astype(jnp.float32)


def unit_kernel(
    query_any, passage_any, own_ref, first_ref, second_ref, scale_ref, query_ref, passage_ref, sems
):
    copies = [
        pltpu.make_async_copy(query_any, query_ref, sems.at[0]),
        pltpu.make_async_copy(passage_any, passage_ref, sems.at[1]),
    ]
    for copy in copies:
        copy.start()
    for copy in copies:
        copy.wait()
    raw_rows = jnp.concatenate(
        [query_ref[...].astype(jnp.float32), passage_ref[...].astype(jnp.float32)], axis=0
    )
    scale_rows = lax.rsqrt(jnp.sum(raw_rows * raw_rows, axis=1, keepdims=True) + EPS)
    low_rows = (raw_rows * scale_rows).astype(jnp.bfloat16)
    width = first_ref.shape[1]
    own_ref[...] = low_rows
    first_ref[...] = low_rows[:, :width]
    second_ref[...] = low_rows[:, width:]
    scale_ref[...] = scale_rows


def unit_rows(query_raw, passage_raw):
    rows, width = query_raw.shape
    whole = jax.ShapeDtypeStruct((2 * rows, width), jnp.bfloat16)
    half = jax.ShapeDtypeStruct((2 * rows, width // 2), jnp.bfloat16)
    return pl.pallas_call(
        unit_kernel,
        in_specs=[HBM, HBM],
        out_specs=(VMEM, VMEM, VMEM, VMEM),
        out_shape=(whole, half, half, jax.ShapeDtypeStruct((2 * rows, 1), jnp.float32)),
        scratch_shapes=[
            pltpu.VMEM((rows, width), jnp.bfloat16),
            pltpu.VMEM((rows, width), jnp.bfloat16),
            pltpu.SemaphoreType.DMA((2,)),
        ],
        compiler_params=pltpu.CompilerParams(vmem_limit_bytes=121 * 2**19),
        cost_estimate=pl.CostEstimate(
            flops=6 * rows * width, bytes_accessed=8 * rows * width, transcendentals=0
        ),
        name="unit_rows",
    )(query_raw, passage_raw)


def score_call(body, name, count, outs, operands, passed=()):
    size = sum(operand.size for operand in operands)
    return pl.pallas_call(
        body,
        in_specs=[VMEM] * len(operands),
        out_specs=[VMEM] * (len(outs) + len(passed)),
        out_shape=[jax.ShapeDtypeStruct(shape, jnp.float32) for shape in outs]
        + [jax.ShapeDtypeStruct(value.shape, value.dtype) for value in passed],
        compiler_params=pltpu.CompilerParams(vmem_limit_bytes=16 * 2**20),
        cost_estimate=pl.CostEstimate(
            flops=2 * count * size, bytes_accessed=2 * size, transcendentals=count * count
        ),
        name=name,
    )(*operands)


def halves_score(own, first, second):
    width = first.shape[1]
    return contract(own[:, :width], first) + contract(own[:, width:], second)


def early_kernel(
    partner_ref, own_ref, near_ref, next_first, next_second, *outs
):
    *score_outs, mass_ref, blank_ref, passed_ref = outs
    partner = partner_ref[...]
    count = partner.shape[0]
    down = lax.broadcasted_iota(jnp.int32, (count, count), 0)
    keep = 1.0 - eye_of(count) - jnp.where(down >= count // 2, partner, 0.0)
    own = own_ref[...]
    scores = [
        contract(own, own),
        contract(own, near_ref[...]),
        halves_score(own, next_first[...], next_second[...]),
    ]
    mass = exp_score(scores[0]) * keep
    for score in scores[1:]:
        mass = mass + exp_score(score)
    for score, score_out in zip(scores, score_outs):
        score_out[...] = score
    mass_ref[...] = mass
    blank_ref[...] = jnp.zeros((count, count), jnp.float32)
    passed_ref[...] = next_first[...]


def far_kernel(place, own_ref, far_ref, sum_ref, score_ref):
    width = far_ref.shape[1]
    own = own_ref[:, place * width : (place + 1) * width]
    score_ref[...] = sum_ref[...] + contract(own, far_ref[...])


def far_scores(own, far, score_sum, place):
    count = own.shape[0]
    body = functools.partial(far_kernel, place)
    return score_call(body, "far_scores", count, [(count, count)], [own, far, score_sum])[0]


def side_kernel(place, sum_ref, own_ref, key_ref, sum_out, score_out):
    width = key_ref.shape[1]
    sum_out[...] = sum_ref[...]
    score_out[...] = contract(own_ref[:, place * width : (place + 1) * width], key_ref[...])


def side_scores(own, key, score_sum, place):
    count = own.shape[0]
    body = functools.partial(side_kernel, place)
    return score_call(body, "side_scores", count, [(count, count)] * 2, [score_sum, own, key])


def total_kernel(
    far_score_ref, mass_ref, score_ref, partner_ref, own_ref, own_mate_score, near_mate_ref, mate_first, mate_second,
    near_mate_out, next_mate_out, recip_ref, spread_ref, loss_ref,
):
    partner = partner_ref[...]
    own = own_ref[...]
    mass = mass_ref[...] + exp_score(far_score_ref[...])
    mass = mass + exp_score(own_mate_score[...])
    near_score = contract(own, near_mate_ref[...])
    near_mate_out[...] = near_score
    mass = mass + exp_score(near_score)
    next_score = halves_score(own, mate_first[...], mate_second[...])
    next_mate_out[...] = next_score
    mass = mass + exp_score(next_score)
    total_col = jnp.sum(mass, axis=1, keepdims=True)
    eye = eye_of(partner.shape[0])
    norm_row = jnp.sum((eye + partner) * total_col, axis=0, keepdims=True)
    recip_ref[...] = 1.0 / norm_row
    spread_ref[...] = jnp.broadcast_to(1.0 / norm_row, spread_ref.shape)
    positive = jnp.sum(partner * score_ref[...], axis=0, keepdims=True)
    losses = jnp.log(norm_row) + INV_TEMP - INV_TEMP * positive
    loss_ref[...] = losses[:, : loss_ref.shape[1]]


def weigh(score, recip_col, recip_row):
    weight = exp_score(score) * (recip_col + recip_row)
    low = weight.astype(jnp.bfloat16)
    return low, low.astype(jnp.float32) * score


def column_of(row):
    return jnp.sum(eye_of(row.shape[1]) * row, axis=1, keepdims=True)


def part_kernel(
    partner_ref, own_row, mate_row, even_row, next_rows, own_score, mate_score, next_score, next_mate_score,
    own_ref, mate_ref, next_0, next_1, pair_0, pair_1, sum_ref, along_ref, passed_ref,
):
    partner = partner_ref[...]
    count = partner.shape[0]
    recip_row = own_row[...]
    recip_col = column_of(recip_row)
    score = own_score[...]
    weight = exp_score(score) * (recip_col + recip_row)
    weight = weight * (1.0 - eye_of(count)) * (1.0 - 0.5 * partner) - partner
    low = weight.astype(jnp.bfloat16)
    weights = [low]
    along = low.astype(jnp.float32) * score
    for score_ref, row in (
        (mate_score, mate_row[...]),
        (next_score, next_rows[0:1, :]),
        (next_mate_score, next_rows[1:2, :]),
    ):
        low, share = weigh(score_ref[...], recip_col, row)
        weights.append(low)
        along = along + share
    along_ref[...] = along
    passed_ref[...] = even_row[0:1, :]
    weights = jnp.concatenate(weights, axis=1)
    half = next_0.shape[1]
    for start in range(0, own_ref.shape[1], TILE):
        whole = slice(start, start + TILE)
        columns = slice(start % half, start % half + TILE)
        next_ref, pair_ref = ((next_0, pair_0), (next_1, pair_1))[start // half]
        keys = [
            own_ref[:, whole],
            mate_ref[:, whole],
            next_ref[:, columns],
            pair_ref[:, columns],
        ]
        keys = jnp.concatenate(keys, axis=0)
        sum_ref[:, whole] = jnp.dot(weights, keys, preferred_element_type=jnp.float32)


def part_gradients(partner, rows, scores, keys):
    count = partner.shape[0]
    width = keys[0].shape[1]
    operands = [partner, *rows, *scores, *keys]
    return pl.pallas_call(
        part_kernel,
        in_specs=[VMEM] * len(operands),
        out_specs=(VMEM, VMEM, VMEM),
        out_shape=(
            jax.ShapeDtypeStruct((count, width), jnp.float32),
            jax.ShapeDtypeStruct((count, count), jnp.float32),
            jax.ShapeDtypeStruct((1, count), jnp.float32),
        ),
        compiler_params=pltpu.CompilerParams(vmem_limit_bytes=24 * 2**20),
        cost_estimate=pl.CostEstimate(
            flops=8 * count * count * width,
            bytes_accessed=12 * count * width,
            transcendentals=4 * count * count,
        ),
        name="part_gradients",
    )(*operands)


def gradient_kernel(
    sum_ref, along_ref, scale_ref, own_row, near_rows, even_row, odd_row, near_score, pair_score, far_score,
    near_ref, pair_ref, far_first, far_0, far_1, query_ref, passage_ref,
    query_out, passage_out, query_hold, passage_hold, sems,
):
    count = along_ref.shape[0]
    rows = count // 2
    recip_col = column_of(own_row[...])
    near_low, near_share = weigh(near_score[...], recip_col, near_rows[0:1, :])
    pair_low, pair_share = weigh(pair_score[...], recip_col, near_rows[1:2, :])
    far_low, far_share = weigh(far_score[...], recip_col, even_row[...] + odd_row[...])
    along = along_ref[...] + near_share + pair_share + far_share
    along = INV_TEMP * jnp.sum(along, axis=1, keepdims=True)
    weights = jnp.concatenate([near_low, pair_low, far_low], axis=1)
    half = far_0.shape[1]
    scale = scale_ref[...]
    copies = []
    for start in range(0, near_ref.shape[1], TILE):
        whole = slice(start, start + TILE)
        far_ref = (far_0, far_1)[start // half]
        far = far_first[:, whole] + far_ref[:, start % half : start % half + TILE]
        keys = jnp.concatenate([near_ref[:, whole], pair_ref[:, whole], far], axis=0)
        gradient = jnp.dot(weights, keys, preferred_element_type=jnp.float32) + sum_ref[:, whole]
        for part, raw_ref, hold, out in (
            (0, query_ref, query_hold, query_out),
            (1, passage_ref, passage_hold, passage_out),
        ):
            span = slice(part * rows, (part + 1) * rows)
            unit = raw_ref[:, whole].astype(jnp.float32) * scale[span]
            hold[:, whole] = (INV_TEMP * gradient[span] - unit * along[span]) * scale[span]
            copy = pltpu.make_async_copy(
                hold.at[:, whole], out.at[:, whole], sems.at[len(copies)]
            )
            copy.start()
            copies.append(copy)
    for copy in copies:
        copy.wait()


def gradients(part_sum, along, scale, rows, scores, keys, query_raw, passage_raw):
    count, width = part_sum.shape
    out = jax.ShapeDtypeStruct((count // 2, width), jnp.float32)
    operands = [part_sum, along, scale, *rows, *scores, *keys, query_raw, passage_raw]
    return pl.pallas_call(
        gradient_kernel,
        in_specs=[VMEM] * len(operands),
        out_specs=(HBM, HBM),
        out_shape=(out, out),
        scratch_shapes=[
            pltpu.VMEM((count // 2, width), jnp.float32),
            pltpu.VMEM((count // 2, width), jnp.float32),
            pltpu.SemaphoreType.DMA((2 * width // TILE,)),
        ],
        compiler_params=pltpu.CompilerParams(vmem_limit_bytes=24 * 2**20),
        cost_estimate=pl.CostEstimate(
            flops=6 * count * count * width,
            bytes_accessed=16 * count * width,
            transcendentals=3 * count * count,
        ),
        name="gradients",
    )(*operands)


def per_device(query_raw, passage_raw, pairing):
    size = lax.axis_size("dp")
    chips = size // 2
    rows = query_raw.shape[0]

    def swapped(value, partner_of):
        pairs = []
        for source in range(size):
            target = partner_of(source // 2, source % 2)
            if target is not None:
                pairs.append((source, (target[0] % chips) * 2 + target[1]))
        return lax.ppermute(value, "dp", pairs)

    def other_core(chip, core):
        return (chip, 1 - core)

    def near_chip(chip, core):
        return (chip ^ 1, core)

    def next_chip(chip, core):
        return (chip + 1 if chip % 2 else chip - 1, core)

    def far_over_next(chip, core):
        return (chip + 1 if core else chip - 1, 1 - core) if chip % 2 == core else None

    def far_over_near(chip, core):
        return (chip + 1 if core else chip - 1, 1 - core) if chip % 2 != core else None

    def beyond_of(parity, chip, core):
        return (chip + 2 if core else chip - 2, 1 - core) if chip % 2 == parity else None

    own, first, second, scale = unit_rows(query_raw, passage_raw)
    paired = (pairing[0][:, None] == jnp.arange(rows, dtype=jnp.int32)[None, :]).astype(jnp.float32)
    blank = jnp.zeros((rows, rows), jnp.float32)
    partner = jnp.block([[blank, paired], [paired.T, blank]])

    near = swapped(own, near_chip)
    next_halves = [swapped(half, next_chip) for half in (first, second)]
    mate = swapped(own, other_core)
    far_first = swapped(near, far_over_next)
    far_second = [swapped(half, far_over_near) for half in next_halves]
    near_mate = swapped(near, other_core)

    count = 2 * rows
    square = (count, count)
    *scores, mass, far_score, passed = score_call(
        early_kernel,
        "early_scores",
        count,
        [square] * 5,
        [partner, own, near, *next_halves],
        [next_halves[0]],
    )
    next_mate = [swapped(half, other_core) for half in (passed, next_halves[1])]
    far_score = far_scores(own, far_second[0], far_score, 0)
    far_score, mate_score = side_scores(own, mate, far_score, 0)
    far_score = far_scores(own, far_second[1], far_score, 1)
    far_score = far_scores(own, far_first, far_score, 0)
    near_mate_score, next_mate_score, recip, spread, losses = score_call(
        total_kernel,
        "totals",
        count,
        [square, square, (1, count), (SPREAD, count), (1, rows)],
        [far_score, mass, scores[0], partner, own, mate_score, near_mate, *next_mate],
    )

    mate_row = swapped(recip, other_core)
    chip_rows = jnp.concatenate([recip, mate_row], axis=0)
    near_rows = swapped(chip_rows, near_chip)
    next_rows = swapped(chip_rows, next_chip)
    even_row = swapped(spread, functools.partial(beyond_of, 0))
    odd_row = swapped(recip, functools.partial(beyond_of, 1))

    near_score, next_score = scores[1:]
    part_sum, along, even_row = part_gradients(
        partner,
        [recip, mate_row, even_row, next_rows],
        [scores[0], mate_score, next_score, next_mate_score],
        [own, mate, *next_halves, *next_mate],
    )
    query_grad, passage_grad = gradients(
        part_sum,
        along,
        scale,
        [recip, near_rows, even_row, odd_row],
        [near_score, near_mate_score, far_score],
        [near, near_mate, far_first, *far_second],
        query_raw,
        passage_raw,
    )
    return (losses.reshape(rows), query_grad, passage_grad)


def solution(mesh):
    in_specs = (P("dp", None), P("dp", None), P("dp", None))
    out_specs = (P("dp"), P("dp", None), P("dp", None))
    return jax.shard_map(
        per_device, mesh=mesh, in_specs=in_specs, out_specs=out_specs, check_vma=False
    )
```
